128 devices in a mesh: grp: 4 (over z_hi, core), seq: 32 (over z_lo, x, y).
Axes of the slice: x: 4, y: 4, z: 4 (z_hi: 2, z_lo: 2; z = z_hi * 2 + z_lo), core: 2. Of those that a mesh axis runs over, the one named last changes fastest.
Arguments:
- comp_q: bfloat16 [4, 4096, 4096], P('grp', 'seq'), may hold values from -136 to 136
- comp_k: bfloat16 [4, 4096, 4096], P('grp', 'seq'), may hold values from -4.5 to 4.5
- comp_v: bfloat16 [4, 4096, 4096], P('grp', 'seq'), may hold values from -6 to 6
- cotangent: bfloat16 [4, 4096, 4096], P('grp', 'seq'), may hold values from -6 to 6
- prompt_k: bfloat16 [4, 2048, 4096], P('grp', 'seq'), may hold values from -6 to 6
- prompt_v: bfloat16 [4, 2048, 4096], P('grp', 'seq'), may hold values from -6 to 6
- lengths: int32 [4, 4], P('grp'), may hold values from 128 to 1024, as said below
- loss_mask: int32 [4, 4096], P('grp', 'seq'), may hold values 0 or 1
- advantage: float32 [4, 4], P('grp'), may hold values from -4 to 4
Outputs:
- grad_q: bfloat16 [4, 4096, 4096], P('grp', 'seq')
- grad_k: bfloat16 [4, 4096, 4096], P('grp', 'seq')
- grad_v: bfloat16 [4, 4096, 4096], P('grp', 'seq')
- grad_prompt_k: bfloat16 [4, 2048, 4096], P('grp', 'seq')
- grad_prompt_v: bfloat16 [4, 2048, 4096], P('grp', 'seq')
The draws below stay inside these ranges and needn't reach their ends.
Inputs may be any that keep to these rules, and one draw needn't show every extreme that they name: `lengths`: multiples of 128; in every group some completion has length 1024.
All inputs are finite; a program needn't handle non-finite values. No bound on the sum of `loss_mask` on one device may be relied on, other than what follows from the above.
Results may differ from the reference program's by a relative error of at most 0.0099.
Values may be sent and summed in bfloat16 or wider, within the bound.
No kernel may reach another device: no remote copies, remote signals or barrier semaphores. Data moves between devices by JAX's collectives and lax.ppermute only.
A program may use at most 128 MiB of HBM per device.

```python
import jax
import jax.numpy as jnp
from jax import lax

HEADS = 32
HEAD_DIM = 128
D = 4096
BUCKET = 128
BUCKETS = 8
LMAX = 1024
PROMPT = 2048
CTOK = 4096
COMP = 4
GROUPS = 4


def shared_keys(key):
    return jnp.clip(jax.random.normal(key, (GROUPS, CTOK, D), jnp.float32), -4.5, 4.5)


def draw_comp_k(key, part):
    shared = shared_keys(key)
    return shared.astype(jnp.bfloat16)


def draw_comp_q(key, part):
    key = jax.random.fold_in(key, 2)
    first = jax.random.fold_in(key, 0)
    fresh = jnp.clip(jax.random.normal(first, (GROUPS, CTOK, D), jnp.float32), -4.5, 4.5)
    return fresh.astype(jnp.bfloat16)


def draw_lengths(key, part):
    key = jax.random.fold_in(key, 3)
    first, second = jax.random.split(key)
    steps = jax.random.randint(first, (GROUPS, COMP), 1, BUCKETS + 1)
    chosen = jax.random.randint(second, (GROUPS, 1), 0, COMP)
    steps = jnp.where(jnp.arange(COMP)[None, :] == chosen, BUCKETS, steps)
    return (steps * BUCKET).astype(jnp.int32)


def with_ends(values, own_key, smallest, high):
    longest = values.shape.index(max(values.shape))
    spots = []
    for shift in (0, 1):
        where = [jax.random.randint(jax.random.fold_in(own_key, axis), (), 0, length) for axis, length in enumerate(values.shape)]
        where[longest] = (where[longest] + shift) % values.shape[longest]
        spots.append(tuple(where))
    return values.at[spots[0]].set(smallest).at[spots[1]].set(high)


def steps_of(key, dims, shards, smallest, largest):
    factor_of, own = 1.0, jax.random.fold_in(key, 6)
    for dim, blocks in shards:
        heights = jnp.exp(jax.random.uniform(jax.random.fold_in(own, dim), (blocks,), jnp.float32, smallest / len(shards), largest / len(shards)))
        factor_of = factor_of * jnp.repeat(heights, dims[dim] // blocks).reshape([-1 if axis == dim else 1 for axis in range(len(dims))])
    return factor_of


def bell_draw(rng, extent, width, reach, shards=(), kind=jnp.bfloat16):
    result = jax.random.normal(rng, extent, jnp.float32) * width
    if len(shards) > 0:
        result = steps_of(rng, extent, shards, -0.22, 0.18) * result
    return jnp.clip(result, min=-reach, max=reach).astype(kind)


def setup_inputs(seed: int = 0) -> dict:
    keys = jax.random.split(jax.random.key(seed), 10)
    return {
        "comp_q": draw_comp_q(jax.random.fold_in(keys[9], 71), 0),
        "comp_k": draw_comp_k(jax.random.fold_in(keys[9], 71), 0),
        "comp_v": bell_draw(keys[2], (GROUPS, CTOK, D), 1.0, 6.0, ((0, 4), (1, 32))),
        "cotangent": bell_draw(keys[3], (GROUPS, CTOK, D), 1.0, 6.0, ((0, 4), (1, 32))),
        "prompt_k": bell_draw(keys[4], (GROUPS, PROMPT, D), 1.0, 6.0, ((0, 4), (1, 32))),
        "prompt_v": bell_draw(keys[5], (GROUPS, PROMPT, D), 1.0, 6.0, ((0, 4), (1, 32))),
        "lengths": draw_lengths(jax.random.fold_in(keys[9], 71), 0),
        "loss_mask": with_ends((jax.random.randint(keys[7], (GROUPS, CTOK), 0, 4) < 3).astype(jnp.int32), jax.random.fold_in(keys[7], 1), 0, 1),
        "advantage": bell_draw(keys[8], (GROUPS, COMP), 1.0, 4.0, ((0, 4),), jnp.float32),
    }


def slot_grads(queries, keys_c, values_c, grad_out, keys_p, values_p, length):
    temper = HEAD_DIM ** -0.5
    all_keys = jnp.concatenate([keys_p, keys_c], axis=0)
    all_values = jnp.concatenate([values_p, values_c], axis=0)
    visible = jnp.concatenate([jnp.ones((keys_p.shape[0],), bool), jnp.arange(keys_c.shape[0]) < length])
    scores = jnp.dot(queries, all_keys.T, preferred_element_type=jnp.float32) * temper
    scores = jnp.where(visible[None, :], scores, -1e30)
    row_peak = jnp.max(scores, axis=1, keepdims=True)
    expo = jnp.exp(scores - row_peak)
    attn_prob = expo / jnp.sum(expo, axis=1, keepdims=True)
    prob_low = attn_prob.astype(jnp.bfloat16)
    attended = jnp.dot(prob_low, all_values, preferred_element_type=jnp.float32)
    row_delta = jnp.sum(grad_out.astype(jnp.float32) * attended, axis=1, keepdims=True)
    grad_values = jnp.dot(prob_low.T, grad_out, preferred_element_type=jnp.float32)
    grad_prob = jnp.dot(grad_out, all_values.T, preferred_element_type=jnp.float32)
    grad_scores = (attn_prob * (grad_prob - row_delta)).astype(jnp.bfloat16)
    grad_query = jnp.dot(grad_scores, all_keys, preferred_element_type=jnp.float32) * temper
    grad_keys = jnp.dot(grad_scores.T, queries, preferred_element_type=jnp.float32) * temper
    split_at = keys_p.shape[0]
    return grad_query, grad_keys[split_at:], grad_values[split_at:], grad_keys[:split_at], grad_values[:split_at]


def heads_of(matrix):
    return matrix.reshape(matrix.shape[0], HEADS, HEAD_DIM).transpose(1, 0, 2)


def group_grads(queries, keys_c, values_c, grad_out, keys_p, values_p, slot_lengths):
    def one_head(items):
        q_head, k_head, v_head, d_head, kp_head, vp_head = items

        def advance(running, inputs_now):
            q_slot, k_slot, v_slot, d_slot, slot_len = inputs_now
            grad_qs, grad_ks, grad_vs, grad_kp, grad_vp = slot_grads(q_slot, k_slot, v_slot, d_slot, kp_head, vp_head, slot_len)
            return (running[0] + grad_kp, running[1] + grad_vp), (grad_qs.astype(jnp.bfloat16), grad_ks.astype(jnp.bfloat16), grad_vs.astype(jnp.bfloat16))

        shaped = tuple(item.reshape(COMP, LMAX, HEAD_DIM) for item in (q_head, k_head, v_head, d_head))
        start = (jnp.zeros((PROMPT, HEAD_DIM), jnp.float32), jnp.zeros((PROMPT, HEAD_DIM), jnp.float32))
        sums, results = lax.scan(advance, start, shaped + (slot_lengths,))
        flat = tuple(item.reshape(CTOK, HEAD_DIM) for item in results)
        return flat + (sums[0].astype(jnp.bfloat16), sums[1].astype(jnp.bfloat16))

    outputs = lax.map(one_head, tuple(heads_of(item) for item in (queries, keys_c, values_c, grad_out, keys_p, values_p)))
    return tuple(item.transpose(1, 0, 2).reshape(item.shape[1], D) for item in outputs)


def reference(comp_q, comp_k, comp_v, cotangent, prompt_k, prompt_v, lengths, loss_mask, advantage):
    token_ids = jnp.arange(CTOK, dtype=jnp.int32)
    slot_ids = token_ids // LMAX
    position = token_ids % LMAX
    live = position[None, :] < lengths[:, slot_ids]
    live_weight = loss_mask * live.astype(jnp.int32)
    live_total = jnp.sum(live_weight.astype(jnp.float32))
    loss_scale = (GROUPS * CTOK) / jnp.maximum(live_total, 1.0)
    factor = advantage[:, slot_ids] * live_weight.astype(jnp.float32) * loss_scale
    grad_out = (cotangent.astype(jnp.float32) * factor[:, :, None]).astype(jnp.bfloat16)
    collected = [[], [], [], [], []]
    for group in range(GROUPS):
        parts = group_grads(comp_q[group], comp_k[group], comp_v[group], grad_out[group], prompt_k[group], prompt_v[group], lengths[group])
        for index in range(5):
            collected[index].append(parts[index])
    return (jnp.stack(collected[0]), jnp.stack(collected[1]), jnp.stack(collected[2]), jnp.stack(collected[3]), jnp.stack(collected[4]))
```

```python
import jax
import jax.numpy as jnp
from jax import lax
from jax.experimental import pallas as pl
from jax.experimental.pallas import tpu as pltpu
from jax.sharding import PartitionSpec as P

HEADS = 32
HEAD_DIM = 128
LMAX = 1024
PROMPT = 2048
COMP = 4
BUCKET = 128
PROWS = 64
KEYS = PROMPT + LMAX
QB = 256
QSTEPS = LMAX // QB
CHUNK = 512
TEMPER = HEAD_DIM ** (-0.5)
LOG2E = 1.4426950408889634
HIDDEN = -1e30

Q0, K0, D0, KP0, ROWS1 = 0, 128, 256, 384, 448
V0, VP0, CNT0, ROWS2 = 0, 128, 192, 200
DV0, DVP0, ROWS3 = 0, 128, 192
DK0, DQ0, DKP0, ROWS4 = 0, 128, 256, 320

NT = (((1,), (1,)), ((), ()))
NN = (((1,), (0,)), ((), ()))


def dot(left, right, dims):
    return lax.dot_general(left, right, dims, preferred_element_type=jnp.float32)


def rows_of(ref, first, count, low, high):
    return ref[pl.ds(first, count), low:high, :].reshape(count * (high - low), HEAD_DIM)


def key_chunks(ref, slot, comp_low, prompt_low):
    per_prompt, per_comp = CHUNK // PROWS, CHUNK // BUCKET
    for index in range(PROMPT // CHUNK):
        yield index * CHUNK, rows_of(ref, index * per_prompt, per_prompt, prompt_low, prompt_low + PROWS)
    for index in range(LMAX // CHUNK):
        yield (
            PROMPT + index * CHUNK,
            rows_of(ref, slot * 8 + index * per_comp, per_comp, comp_low, comp_low + BUCKET),
        )


def fold(values, op):
    return op(values.reshape(values.shape[0] // 8, 8, values.shape[1]), axis=0)


def prob_kernel(len_ref, x_ref, p_ref, o_ref, s_ref, acc_p, acc_c):
    slot, step = pl.program_id(0), pl.program_id(1)
    length = len_ref[slot]

    @pl.when((slot == 0) & (step == 0))
    def _():
        acc_p[...] = jnp.zeros_like(acc_p)

    @pl.when(step == 0)
    def _():
        acc_c[...] = jnp.zeros_like(acc_c)

    @pl.when(step * QB < length)
    def _():
        mine = slot * 8 + step * (QB // BUCKET)
        queries = rows_of(x_ref, mine, QB // BUCKET, Q0, Q0 + BUCKET)
        grad_out = rows_of(x_ref, mine, QB // BUCKET, D0, D0 + BUCKET)
        peak = jnp.full((8, QB), HIDDEN, jnp.float32)
        for first, keys in key_chunks(x_ref, slot, K0, KP0):
            scores = dot(keys, queries, NT) * (TEMPER * LOG2E)
            if first >= PROMPT:
                parts = []
                for low in range(0, CHUNK, BUCKET):
                    seen = first - PROMPT + low < length
                    parts.append(jnp.where(seen, scores[low : low + BUCKET], HIDDEN))
                scores = jnp.concatenate(parts, axis=0)
            s_ref[first : first + CHUNK, :] = scores
            peak = jnp.maximum(peak, fold(scores, jnp.max))
        top = jnp.max(peak, axis=0, keepdims=True)
        total = jnp.zeros((8, QB), jnp.float32)
        for first in range(0, KEYS, CHUNK):
            expo = jnp.exp2(s_ref[first : first + CHUNK, :] - top)
            s_ref[first : first + CHUNK, :] = expo
            total = total + fold(expo, jnp.sum)
        inverse = 1.0 / jnp.sum(total, axis=0, keepdims=True)
        for first in range(0, KEYS, CHUNK):
            prob = (s_ref[first : first + CHUNK, :] * inverse).astype(jnp.bfloat16)
            p_ref[0, 0, first : first + CHUNK, :] = prob
            grad = dot(prob, grad_out, NN)
            if first < PROMPT:
                acc_p[first : first + CHUNK, :] += grad
            else:
                acc_c[first - PROMPT : first - PROMPT + CHUNK, :] += grad

    @pl.when(step == QSTEPS - 1)
    def _():
        o_ref[pl.ds(slot * 8, 8), DV0 : DV0 + BUCKET, :] = (
            acc_c[...].astype(jnp.bfloat16).reshape(8, BUCKET, HEAD_DIM)
        )

    @pl.when((slot == COMP - 1) & (step == QSTEPS - 1))
    def _():
        o_ref[:, DVP0 : DVP0 + PROWS, :] = (
            acc_p[...].astype(jnp.bfloat16).reshape(HEADS, PROWS, HEAD_DIM)
        )


def score_kernel(len_ref, x_ref, y_ref, p_ref, o_ref, s_ref, acc_p, acc_c, kpt_ref, kct_ref):
    slot, step = pl.program_id(0), pl.program_id(1)
    length = len_ref[slot]

    @pl.when((slot == 0) & (step == 0))
    def _():
        acc_p[...] = jnp.zeros_like(acc_p)
        kpt_ref[...] = rows_of(x_ref, 0, HEADS, KP0, KP0 + PROWS).T

    @pl.when(step == 0)
    def _():
        acc_c[...] = jnp.zeros_like(acc_c)
        kct_ref[...] = rows_of(x_ref, slot * 8, 8, K0, K0 + BUCKET).T

    mine = slot * 8 + step * (QB // BUCKET)

    @pl.when(step * QB < length)
    def _():
        queries = rows_of(x_ref, mine, QB // BUCKET, Q0, Q0 + BUCKET)
        grad_out = rows_of(x_ref, mine, QB // BUCKET, D0, D0 + BUCKET)
        partial = jnp.zeros((8, QB), jnp.float32)
        for first, values in key_chunks(y_ref, slot, V0, VP0):
            grad_prob = dot(values, grad_out, NT)
            s_ref[first : first + CHUNK, :] = grad_prob
            prob = p_ref[0, 0, first : first + CHUNK, :].astype(jnp.float32)
            partial = partial + fold(prob * grad_prob, jnp.sum)
        delta = jnp.sum(partial, axis=0, keepdims=True)
        grad_q = jnp.zeros((HEAD_DIM, QB), jnp.float32)
        for first in range(0, KEYS, CHUNK):
            prob = p_ref[0, 0, first : first + CHUNK, :].astype(jnp.float32)
            grad_s = (prob * (s_ref[first : first + CHUNK, :] - delta)).astype(jnp.bfloat16)
            grad = dot(grad_s, queries, NN)
            if first < PROMPT:
                acc_p[first : first + CHUNK, :] += grad
                grad_q = grad_q + dot(kpt_ref[:, first : first + CHUNK], grad_s, NN)
            else:
                low = first - PROMPT
                acc_c[low : low + CHUNK, :] += grad
                grad_q = grad_q + dot(kct_ref[:, low : low + CHUNK], grad_s, NN)
        o_ref[pl.ds(mine, QB // BUCKET), DQ0 : DQ0 + BUCKET, :] = (
            (grad_q.T * TEMPER).astype(jnp.bfloat16).reshape(QB // BUCKET, BUCKET, HEAD_DIM)
        )

    @pl.when(step * QB >= length)
    def _():
        o_ref[pl.ds(mine, QB // BUCKET), DQ0 : DQ0 + BUCKET, :] = jnp.zeros(
            (QB // BUCKET, BUCKET, HEAD_DIM), jnp.bfloat16
        )

    @pl.when(step == QSTEPS - 1)
    def _():
        o_ref[pl.ds(slot * 8, 8), DK0 : DK0 + BUCKET, :] = (
            (acc_c[...] * TEMPER).astype(jnp.bfloat16).reshape(8, BUCKET, HEAD_DIM)
        )

    @pl.when((slot == COMP - 1) & (step == QSTEPS - 1))
    def _():
        o_ref[:, DKP0 : DKP0 + PROWS, :] = (
            (acc_p[...] * TEMPER).astype(jnp.bfloat16).reshape(HEADS, PROWS, HEAD_DIM)
        )


def whole(rows):
    return pl.BlockSpec((HEADS, rows, HEAD_DIM), lambda slot, step, lens: (0, 0, 0))


PROB_SPEC = pl.BlockSpec((1, 1, KEYS, QB), lambda slot, step, lens: (slot, step, 0, 0))
PRODUCT = 2 * COMP * LMAX * KEYS * HEAD_DIM


def run_prob(lengths, first):
    return pl.pallas_call(
        prob_kernel,
        grid_spec=pltpu.PrefetchScalarGridSpec(
            num_scalar_prefetch=1,
            grid=(COMP, QSTEPS),
            in_specs=[whole(ROWS1)],
            out_specs=[PROB_SPEC, whole(ROWS3)],
            scratch_shapes=[
                pltpu.VMEM((KEYS, QB), jnp.float32),
                pltpu.VMEM((PROMPT, HEAD_DIM), jnp.float32),
                pltpu.VMEM((LMAX, HEAD_DIM), jnp.float32),
            ],
        ),
        out_shape=[
            jax.ShapeDtypeStruct((COMP, QSTEPS, KEYS, QB), jnp.bfloat16),
            jax.ShapeDtypeStruct((HEADS, ROWS3, HEAD_DIM), jnp.bfloat16),
        ],
        compiler_params=pltpu.CompilerParams(
            dimension_semantics=("arbitrary", "arbitrary"), vmem_limit_bytes=40 * 2**20
        ),
        cost_estimate=pl.CostEstimate(
            flops=2 * PRODUCT, bytes_accessed=30 * 2**20, transcendentals=COMP * LMAX * KEYS
        ),
        name="attn_prob",
    )(lengths, first)


def run_score(lengths, first, second, prob):
    return pl.pallas_call(
        score_kernel,
        grid_spec=pltpu.PrefetchScalarGridSpec(
            num_scalar_prefetch=1,
            grid=(COMP, QSTEPS),
            in_specs=[whole(ROWS1), whole(ROWS2), PROB_SPEC],
            out_specs=whole(ROWS4),
            scratch_shapes=[
                pltpu.VMEM((KEYS, QB), jnp.float32),
                pltpu.VMEM((PROMPT, HEAD_DIM), jnp.float32),
                pltpu.VMEM((LMAX, HEAD_DIM), jnp.float32),
                pltpu.VMEM((HEAD_DIM, PROMPT), jnp.bfloat16),
                pltpu.VMEM((HEAD_DIM, LMAX), jnp.bfloat16),
            ],
        ),
        out_shape=jax.ShapeDtypeStruct((HEADS, ROWS4, HEAD_DIM), jnp.bfloat16),
        compiler_params=pltpu.CompilerParams(
            dimension_semantics=("arbitrary", "arbitrary"), vmem_limit_bytes=40 * 2**20
        ),
        cost_estimate=pl.CostEstimate(
            flops=3 * PRODUCT, bytes_accessed=30 * 2**20, transcendentals=0
        ),
        name="grad_scores",
    )(lengths, first, second, prob)


def to_heads(matrix):
    return matrix.reshape(matrix.shape[0], HEADS, HEAD_DIM).transpose(1, 0, 2)


def exchange(blocks):
    return lax.all_to_all(blocks, "seq", split_axis=0, concat_axis=0, tiled=True)


def on_device(comp_q, comp_k, comp_v, cotangent, prompt_k, prompt_v, lengths, loss_mask, advantage):
    row_count = comp_q.shape[1]
    seq_ways = lax.axis_size("seq")
    grp_ways = lax.axis_size("grp")
    slot_total = lengths.shape[1]
    token_ids = lax.axis_index("seq") * row_count + jnp.arange(row_count, dtype=jnp.int32)
    slot_ids = token_ids // LMAX
    position = token_ids % LMAX
    member = slot_ids[:, None] == jnp.arange(slot_total, dtype=jnp.int32)[None, :]
    token_limit = jnp.sum(jnp.where(member, lengths[0][None, :], 0), axis=1)
    token_gain = jnp.sum(jnp.where(member, advantage[0][None, :], 0.0), axis=1)
    live_weight = (loss_mask[0] * (position < token_limit).astype(jnp.int32)).astype(jnp.float32)
    weighted = (cotangent[0].astype(jnp.float32) * (token_gain * live_weight)[:, None]).astype(
        jnp.bfloat16
    )
    count = jnp.broadcast_to(
        jnp.sum(live_weight).astype(jnp.bfloat16), (HEADS, ROWS2 - CNT0, HEAD_DIM)
    )
    send_first = jnp.concatenate(
        [to_heads(comp_q[0]), to_heads(comp_k[0]), to_heads(weighted), to_heads(prompt_k[0])], axis=1
    )
    first = exchange(send_first)
    send_second = jnp.concatenate([to_heads(comp_v[0]), to_heads(prompt_v[0]), count], axis=1)
    send_second, first = lax.optimization_barrier((send_second, first))
    second = exchange(send_second)
    prob, send_third = run_prob(lengths[0], first)
    live_total = jnp.sum(second[:, CNT0, 0].astype(jnp.float32)).reshape(1, 1)
    send_third, second = lax.optimization_barrier((send_third, second))
    third = exchange(send_third)
    for other in (1, 2):
        live_total = live_total + lax.ppermute(
            live_total, "grp", [(index, index ^ other) for index in range(grp_ways)]
        )
    loss_scale = grp_ways * seq_ways * row_count / jnp.maximum(live_total[0, 0], 1.0)
    send_fourth = run_score(lengths[0], first, second, prob)
    send_fourth, third = lax.optimization_barrier((send_fourth, third))
    fourth = exchange(send_fourth)

    def to_rows(blocks, low, count):
        part = blocks[:, low : low + count, :].astype(jnp.float32) * loss_scale
        return part.astype(jnp.bfloat16).transpose(1, 0, 2).reshape(1, count, HEADS * HEAD_DIM)

    return (
        to_rows(fourth, DQ0, BUCKET),
        to_rows(fourth, DK0, BUCKET),
        to_rows(third, DV0, BUCKET),
        to_rows(fourth, DKP0, PROWS),
        to_rows(third, DVP0, PROWS),
    )


def solution(mesh):
    return jax.shard_map(
        on_device,
        mesh=mesh,
        in_specs=(
            P("grp", "seq", None),
            P("grp", "seq", None),
            P("grp", "seq", None),
            P("grp", "seq", None),
            P("grp", "seq", None),
            P("grp", "seq", None),
            P("grp", None),
            P("grp", "seq"),
            P("grp", None),
        ),
        out_specs=(
            P("grp", "seq", None),
            P("grp", "seq", None),
            P("grp", "seq", None),
            P("grp", "seq", None),
            P("grp", "seq", None),
        ),
        check_vma=False,
    )
```

```python
import jax
import jax.numpy as jnp
from jax import lax
from jax.experimental import pallas as pl
from jax.experimental.pallas import tpu as pltpu
from jax.sharding import PartitionSpec as P

HEADS = 32
HEAD_DIM = 128
LMAX = 1024
PROMPT = 2048
COMP = 4
BUCKET = 128
PROWS = 64
KEYS = PROMPT + LMAX
QB = 256
QSTEPS = LMAX // QB
CHUNK = 512
FOLD = 16
TEMPER = HEAD_DIM ** (-0.5)
LOG2E = 1.4426950408889634
HIDDEN = -1e30

Q0, K0, D0, KP0, ROWS1 = 0, 128, 256, 384, 448
V0, VP0, CNT0, ROWS2 = 0, 128, 192, 200
DV0, DVP0, ROWS3 = 0, 128, 192
DK0, DQ0, DKP0, ROWS4 = 0, 128, 256, 320

NT = (((1,), (1,)), ((), ()))
NN = (((1,), (0,)), ((), ()))


def dot(left, right, dims):
    return lax.dot_general(left, right, dims, preferred_element_type=jnp.float32)


def rows_of(ref, first, count, low, high):
    return ref[pl.ds(first, count), low:high, :].reshape(count * (high - low), HEAD_DIM)


def fold(values, op):
    return op(values.reshape(values.shape[0] // FOLD, FOLD, values.shape[1]), axis=0)


def block_counts(lens):
    return [lax.div(lens[slot] + (QB - 1), QB) for slot in range(COMP)]


def locate(lens, index):
    counts = block_counts(lens)
    ends, end = [], 0
    for count in counts:
        end = end + count
        ends.append(end)
    index = jnp.clip(index, 0, end - 1)
    slot, base = 0, 0
    for place in range(COMP - 1):
        passed = index >= ends[place]
        slot = slot + passed.astype(jnp.int32)
        base = jnp.where(passed, ends[place], base)
    return slot, index - base


def live_blocks(lens):
    return sum(block_counts(lens))


def over_chunks(body, carry, comp_rows, prompt_rows, slot):
    per_prompt, per_comp = CHUNK // PROWS, CHUNK // BUCKET

    for low in range(0, PROMPT, CHUNK):
        rows = slice(low, low + CHUNK)
        carry = body(rows, rows, prompt_rows(low // PROWS, per_prompt), None, carry)
    for low in range(0, LMAX, CHUNK):
        rows = slice(PROMPT + low, PROMPT + low + CHUNK)
        acc_rows = slice(low, low + CHUNK)
        carry = body(rows, acc_rows, comp_rows(slot * 8 + low // BUCKET, per_comp), low, carry)
    return carry


def prob_kernel(len_ref, x_ref, p_ref, o_ref, s_ref, e_ref, acc_p, acc_c, top_ref, inv_ref):
    step = pl.program_id(0)
    blocks = live_blocks(len_ref)

    @pl.when(step == 2)
    def _():
        for ref in (acc_p, acc_c):
            ref[...] = jnp.zeros_like(ref)

    @pl.when(step < blocks + 2)
    def _():
        slot, place = locate(len_ref, step)
        old_slot, old_place = locate(len_ref, step - 2)
        length = len_ref[slot]
        queries = rows_of(x_ref, slot * 8 + place * (QB // BUCKET), QB // BUCKET, Q0, Q0 + BUCKET)
        grad_out = rows_of(
            x_ref, old_slot * 8 + old_place * (QB // BUCKET), QB // BUCKET, D0, D0 + BUCKET
        )
        top = top_ref[0:1, :]
        inverse = inv_ref[0:1, :]

        def body(rows, acc_rows, keys, low, carry):
            peak, total = carry
            prob = (e_ref[rows, :] * inverse).astype(jnp.bfloat16)
            p_ref[0, rows, :] = prob
            grad = dot(prob, grad_out, NN)
            if low is None:
                acc_p[acc_rows, :] += grad
            else:
                acc_c[old_slot, acc_rows, :] += grad
            expo = jnp.exp2(s_ref[rows, :] - top)
            e_ref[rows, :] = expo
            total = total + fold(expo, jnp.sum)
            scores = dot(keys, queries, NT) * (TEMPER * LOG2E)
            if low is not None:
                parts = []
                for part in range(0, CHUNK, BUCKET):
                    seen = low + part < length
                    parts.append(jnp.where(seen, scores[part : part + BUCKET], HIDDEN))
                scores = jnp.concatenate(parts, axis=0)
            s_ref[rows, :] = scores
            peak = jnp.maximum(peak, fold(scores, jnp.max))
            return peak, total

        peak, total = over_chunks(
            body,
            (jnp.full((FOLD, QB), HIDDEN, jnp.float32), jnp.zeros((FOLD, QB), jnp.float32)),
            lambda first, count: rows_of(x_ref, first, count, K0, K0 + BUCKET),
            lambda first, count: rows_of(x_ref, first, count, KP0, KP0 + PROWS),
            slot,
        )
        top_ref[0:1, :] = jnp.max(peak, axis=0, keepdims=True)
        inv_ref[0:1, :] = 1.0 / jnp.sum(total, axis=0, keepdims=True)

    @pl.when(step == blocks + 1)
    def _():
        for slot in range(COMP):
            o_ref[slot * 8 : slot * 8 + 8, DV0 : DV0 + BUCKET, :] = (
                acc_c[slot].astype(jnp.bfloat16).reshape(8, BUCKET, HEAD_DIM)
            )
        o_ref[:, DVP0 : DVP0 + PROWS, :] = (
            acc_p[...].astype(jnp.bfloat16).reshape(HEADS, PROWS, HEAD_DIM)
        )


def score_kernel(
    len_ref, x_ref, y_ref, p_ref, o_ref, d_ref, h_ref, acc_p, acc_c, dq_ref, kpt_ref, kct_ref, delta_ref
):
    step = pl.program_id(0)
    blocks = live_blocks(len_ref)

    @pl.when(step == 1)
    def _():
        for ref in (acc_p, acc_c):
            ref[...] = jnp.zeros_like(ref)

    @pl.when(step == 0)
    def _():
        o_ref[:, DQ0 : DQ0 + BUCKET, :] = jnp.zeros((HEADS, BUCKET, HEAD_DIM), jnp.bfloat16)
        kpt_ref[...] = rows_of(x_ref, 0, HEADS, KP0, KP0 + PROWS).T
        for slot in range(COMP):
            kct_ref[slot] = rows_of(x_ref, slot * 8, 8, K0, K0 + BUCKET).T

    @pl.when(step < blocks + 1)
    def _():
        slot, place = locate(len_ref, step)
        old_slot, old_place = locate(len_ref, step - 1)
        grad_out = rows_of(x_ref, slot * 8 + place * (QB // BUCKET), QB // BUCKET, D0, D0 + BUCKET)
        old_first = old_slot * 8 + old_place * (QB // BUCKET)
        queries = rows_of(x_ref, old_first, QB // BUCKET, Q0, Q0 + BUCKET)
        delta = delta_ref[0:1, :]
        dq_ref[...] = jnp.zeros_like(dq_ref)

        def body(rows, acc_rows, values, low, partial):
            grad_s = (h_ref[rows, :].astype(jnp.float32) * (d_ref[rows, :] - delta)).astype(jnp.bfloat16)
            grad = dot(grad_s, queries, NN)
            if low is None:
                acc_p[acc_rows, :] += grad
                dq_ref[...] += dot(kpt_ref[:, acc_rows], grad_s, NN)
            else:
                acc_c[old_slot, acc_rows, :] += grad
                dq_ref[...] += dot(kct_ref[old_slot, :, acc_rows], grad_s, NN)
            grad_prob = dot(values, grad_out, NT)
            prob = p_ref[0, rows, :]
            h_ref[rows, :] = prob
            d_ref[rows, :] = grad_prob
            return partial + fold(prob.astype(jnp.float32) * grad_prob, jnp.sum)

        partial = over_chunks(
            body,
            jnp.zeros((FOLD, QB), jnp.float32),
            lambda first, count: rows_of(y_ref, first, count, V0, V0 + BUCKET),
            lambda first, count: rows_of(y_ref, first, count, VP0, VP0 + PROWS),
            slot,
        )
        delta_ref[0:1, :] = jnp.sum(partial, axis=0, keepdims=True)

        @pl.when(step >= 1)
        def _():
            o_ref[pl.ds(old_first, QB // BUCKET), DQ0 : DQ0 + BUCKET, :] = (
                (dq_ref[...].T * TEMPER).astype(jnp.bfloat16).reshape(QB // BUCKET, BUCKET, HEAD_DIM)
            )

    @pl.when(step == blocks)
    def _():
        for slot in range(COMP):
            o_ref[slot * 8 : slot * 8 + 8, DK0 : DK0 + BUCKET, :] = (
                (acc_c[slot] * TEMPER).astype(jnp.bfloat16).reshape(8, BUCKET, HEAD_DIM)
            )
        o_ref[:, DKP0 : DKP0 + PROWS, :] = (
            (acc_p[...] * TEMPER).astype(jnp.bfloat16).reshape(HEADS, PROWS, HEAD_DIM)
        )


MAX_BLOCKS = COMP * QSTEPS
PRODUCT = 2 * COMP * LMAX * KEYS * HEAD_DIM
WHOLE = pl.BlockSpec(memory_space=pltpu.VMEM)


def prob_spec(lag):
    def place(step, lens):
        return jnp.clip(step - lag, 0, live_blocks(lens) - 1), 0, 0

    return pl.BlockSpec((1, KEYS, QB), place)


def run_prob(lengths, first):
    return pl.pallas_call(
        prob_kernel,
        grid_spec=pltpu.PrefetchScalarGridSpec(
            num_scalar_prefetch=1,
            grid=(MAX_BLOCKS + 2,),
            in_specs=[WHOLE],
            out_specs=[prob_spec(2), WHOLE],
            scratch_shapes=[
                pltpu.VMEM((KEYS, QB), jnp.float32),
                pltpu.VMEM((KEYS, QB), jnp.float32),
                pltpu.VMEM((PROMPT, HEAD_DIM), jnp.float32),
                pltpu.VMEM((COMP, LMAX, HEAD_DIM), jnp.float32),
                pltpu.VMEM((8, QB), jnp.float32),
                pltpu.VMEM((8, QB), jnp.float32),
            ],
        ),
        out_shape=[
            jax.ShapeDtypeStruct((MAX_BLOCKS, KEYS, QB), jnp.bfloat16),
            jax.ShapeDtypeStruct((HEADS, ROWS3, HEAD_DIM), jnp.bfloat16),
        ],
        compiler_params=pltpu.CompilerParams(
            dimension_semantics=("arbitrary",), vmem_limit_bytes=28 * 2**20
        ),
        cost_estimate=pl.CostEstimate(
            flops=2 * PRODUCT, bytes_accessed=30 * 2**20, transcendentals=COMP * LMAX * KEYS
        ),
        name="attn_prob",
    )(lengths, first)


def run_score(lengths, first, second, prob):
    return pl.pallas_call(
        score_kernel,
        grid_spec=pltpu.PrefetchScalarGridSpec(
            num_scalar_prefetch=1,
            grid=(MAX_BLOCKS + 1,),
            in_specs=[WHOLE, WHOLE, prob_spec(0)],
            out_specs=WHOLE,
            scratch_shapes=[
                pltpu.VMEM((KEYS, QB), jnp.float32),
                pltpu.VMEM((KEYS, QB), jnp.bfloat16),
                pltpu.VMEM((PROMPT, HEAD_DIM), jnp.float32),
                pltpu.VMEM((COMP, LMAX, HEAD_DIM), jnp.float32),
                pltpu.VMEM((HEAD_DIM, QB), jnp.float32),
                pltpu.VMEM((HEAD_DIM, PROMPT), jnp.bfloat16),
                pltpu.VMEM((COMP, HEAD_DIM, LMAX), jnp.bfloat16),
                pltpu.VMEM((8, QB), jnp.float32),
            ],
        ),
        out_shape=jax.ShapeDtypeStruct((HEADS, ROWS4, HEAD_DIM), jnp.bfloat16),
        compiler_params=pltpu.CompilerParams(
            dimension_semantics=("arbitrary",), vmem_limit_bytes=28 * 2**20
        ),
        cost_estimate=pl.CostEstimate(
            flops=3 * PRODUCT, bytes_accessed=30 * 2**20, transcendentals=0
        ),
        name="grad_scores",
    )(lengths, first, second, prob)


WIDE = 8


def pack_kernel(len_ref, gain_ref, me_ref, mask_ref, q_ref, k_ref, c_ref, kp_ref, o_ref, factor_ref):
    @pl.when(pl.program_id(0) == 0)
    def _():
        slot = lax.div(me_ref[0], LMAX // BUCKET)
        place = (me_ref[0] - slot * (LMAX // BUCKET)) * BUCKET
        live = (mask_ref[...] * (place < len_ref[slot]).astype(jnp.int32)).astype(jnp.float32)
        factor_ref[...] = jnp.broadcast_to(live * gain_ref[slot], (HEAD_DIM, BUCKET)).T

    for head in range(WIDE):
        lanes = slice(head * HEAD_DIM, head * HEAD_DIM + HEAD_DIM)
        o_ref[head, Q0 : Q0 + BUCKET, :] = q_ref[0, :, lanes]
        o_ref[head, K0 : K0 + BUCKET, :] = k_ref[0, :, lanes]
        o_ref[head, D0 : D0 + BUCKET, :] = (
            c_ref[0, :, lanes].astype(jnp.float32) * factor_ref[...]
        ).astype(jnp.bfloat16)
        o_ref[head, KP0 : KP0 + PROWS, :] = kp_ref[0, :, lanes]


def wide_rows(rows):
    return pl.BlockSpec((1, rows, WIDE * HEAD_DIM), lambda step, *_: (0, 0, step))


def wide_heads(rows):
    return pl.BlockSpec((WIDE, rows, HEAD_DIM), lambda step, *_: (step, 0, 0))


def run_pack(lengths, gain, me, mask, queries, keys, cotangent, prompt_keys):
    return pl.pallas_call(
        pack_kernel,
        grid_spec=pltpu.PrefetchScalarGridSpec(
            num_scalar_prefetch=3,
            grid=(HEADS // WIDE,),
            in_specs=[
                pl.BlockSpec((1, BUCKET), lambda step, *_: (0, 0)),
                wide_rows(BUCKET),
                wide_rows(BUCKET),
                wide_rows(BUCKET),
                wide_rows(PROWS),
            ],
            out_specs=wide_heads(ROWS1),
            scratch_shapes=[pltpu.VMEM((BUCKET, HEAD_DIM), jnp.float32)],
        ),
        out_shape=jax.ShapeDtypeStruct((HEADS, ROWS1, HEAD_DIM), jnp.bfloat16),
        compiler_params=pltpu.CompilerParams(
            dimension_semantics=("arbitrary",), vmem_limit_bytes=16 * 2**20
        ),
        name="pack_first",
    )(lengths, gain, me, mask, queries, keys, cotangent, prompt_keys)


def run_unpack(name, blocks, scale, parts):
    def kernel(scale_ref, x_ref, *o_refs):
        for head in range(WIDE):
            lanes = slice(head * HEAD_DIM, head * HEAD_DIM + HEAD_DIM)
            for (low, rows), o_ref in zip(parts, o_refs):
                o_ref[0, :, lanes] = (
                    x_ref[head, low : low + rows, :].astype(jnp.float32) * scale_ref[0]
                ).astype(jnp.bfloat16)

    return pl.pallas_call(
        kernel,
        grid_spec=pltpu.PrefetchScalarGridSpec(
            num_scalar_prefetch=1,
            grid=(HEADS // WIDE,),
            in_specs=[wide_heads(blocks.shape[1])],
            out_specs=[wide_rows(rows) for _, rows in parts],
        ),
        out_shape=[
            jax.ShapeDtypeStruct((1, rows, HEADS * HEAD_DIM), jnp.bfloat16) for _, rows in parts
        ],
        compiler_params=pltpu.CompilerParams(
            dimension_semantics=("arbitrary",), vmem_limit_bytes=16 * 2**20
        ),
        name=name,
    )(scale, blocks)


def to_heads(matrix):
    return matrix.reshape(matrix.shape[0], HEADS, HEAD_DIM).transpose(1, 0, 2)


def exchange(blocks):
    return lax.all_to_all(blocks, "seq", split_axis=0, concat_axis=0, tiled=True)


def on_device(comp_q, comp_k, comp_v, cotangent, prompt_k, prompt_v, lengths, loss_mask, advantage):
    row_count = comp_q.shape[1]
    seq_ways = lax.axis_size("seq")
    grp_ways = lax.axis_size("grp")
    slot_total = lengths.shape[1]
    token_ids = lax.axis_index("seq") * row_count + jnp.arange(row_count, dtype=jnp.int32)
    slot_ids = token_ids // LMAX
    position = token_ids % LMAX
    member = slot_ids[:, None] == jnp.arange(slot_total, dtype=jnp.int32)[None, :]
    token_limit = jnp.sum(jnp.where(member, lengths[0][None, :], 0), axis=1)
    live_weight = (loss_mask[0] * (position < token_limit).astype(jnp.int32)).astype(jnp.float32)
    count = jnp.broadcast_to(
        jnp.sum(live_weight).astype(jnp.bfloat16), (HEADS, ROWS2 - CNT0, HEAD_DIM)
    )
    me = lax.axis_index("seq").astype(jnp.int32).reshape(1)
    send_first = run_pack(
        lengths[0], advantage[0], me, loss_mask, comp_q, comp_k, cotangent, prompt_k
    )
    first = exchange(send_first)
    send_second = jnp.concatenate([to_heads(comp_v[0]), to_heads(prompt_v[0]), count], axis=1)
    send_second, first = lax.optimization_barrier((send_second, first))
    second = exchange(send_second)
    prob, send_third = run_prob(lengths[0], first)
    live_total = jnp.sum(second[:, CNT0, 0].astype(jnp.float32)).reshape(1, 1)
    send_third, second = lax.optimization_barrier((send_third, second))
    third = exchange(send_third)
    for other in (1, 2):
        live_total = live_total + lax.ppermute(
            live_total, "grp", [(index, index ^ other) for index in range(grp_ways)]
        )
    loss_scale = grp_ways * seq_ways * row_count / jnp.maximum(live_total[0, 0], 1.0)
    send_fourth = run_score(lengths[0], first, second, prob)
    send_fourth, third = lax.optimization_barrier((send_fourth, third))
    fourth = exchange(send_fourth)

    loss_scale = loss_scale.astype(jnp.float32).reshape(1)
    grad_v, grad_vp = run_unpack("unpack_third", third, loss_scale, ((DV0, BUCKET), (DVP0, PROWS)))
    grad_k, grad_q, grad_kp = run_unpack(
        "unpack_fourth", fourth, loss_scale, ((DK0, BUCKET), (DQ0, BUCKET), (DKP0, PROWS))
    )
    return grad_q, grad_k, grad_v, grad_kp, grad_vp


def solution(mesh):
    return jax.shard_map(
        on_device,
        mesh=mesh,
        in_specs=(
            P("grp", "seq", None),
            P("grp", "seq", None),
            P("grp", "seq", None),
            P("grp", "seq", None),
            P("grp", "seq", None),
            P("grp", "seq", None),
            P("grp", None),
            P("grp", "seq"),
            P("grp", None),
        ),
        out_specs=(
            P("grp", "seq", None),
            P("grp", "seq", None),
            P("grp", "seq", None),
            P("grp", "seq", None),
            P("grp", "seq", None),
        ),
        check_vma=False,
    )
```

```python
import jax
import jax.numpy as jnp
from jax import lax
from jax.experimental import pallas as pl
from jax.experimental.pallas import tpu as pltpu
from jax.sharding import PartitionSpec as P

HEADS = 32
HEAD_DIM = 128
LMAX = 1024
PROMPT = 2048
COMP = 4
BUCKET = 128
PROWS = 64
KEYS = PROMPT + LMAX
QB = 256
QSTEPS = LMAX // QB
CHUNK = 1024
FOLD = 16
VMEM_LIMIT = 60 * 2**20
PARTS = 4
TEMPER = HEAD_DIM ** (-0.5)
LOG2E = 1.4426950408889634
HIDDEN = -1e30

Q0, K0, D0, KP0, ROWS1 = 0, 128, 256, 384, 448
V0, VP0, CNT0, ROWS2 = 0, 128, 192, 200
DV0, DVP0, ROWS3 = 0, 128, 192
DK0, DQ0, DKP0, ROWS4 = 0, 128, 256, 320

NT = (((1,), (1,)), ((), ()))
NN = (((1,), (0,)), ((), ()))


def dot(left, right, dims):
    return lax.dot_general(left, right, dims, preferred_element_type=jnp.float32)


def rows_of(ref, first, count, low, high):
    return ref[pl.ds(first, count), low:high, :].reshape(count * (high - low), HEAD_DIM)


def fold(values, op):
    return op(values.reshape(values.shape[0] // FOLD, FOLD, values.shape[1]), axis=0)


def block_counts(lens):
    return [lax.div(lens[slot] + (QB - 1), QB) for slot in range(COMP)]


def locate(lens, index):
    counts = block_counts(lens)
    ends, end = [], 0
    for count in counts:
        end = end + count
        ends.append(end)
    index = jnp.clip(index, 0, end - 1)
    slot, base = 0, 0
    for place in range(COMP - 1):
        passed = index >= ends[place]
        slot = slot + passed.astype(jnp.int32)
        base = jnp.where(passed, ends[place], base)
    return slot, index - base


def live_blocks(lens):
    return sum(block_counts(lens))


def over_chunks(body, carry, comp_rows, prompt_rows, slot):
    per_prompt, per_comp = CHUNK // PROWS, CHUNK // BUCKET

    for low in range(0, PROMPT, CHUNK):
        rows = slice(low, low + CHUNK)
        carry = body(rows, rows, prompt_rows(low // PROWS, per_prompt), None, carry)
    for low in range(0, LMAX, CHUNK):
        rows = slice(PROMPT + low, PROMPT + low + CHUNK)
        acc_rows = slice(low, low + CHUNK)
        carry = body(rows, acc_rows, comp_rows(slot * 8 + low // BUCKET, per_comp), low, carry)
    return carry


def put_blocks(o_ref, first, slots, slot, factor=None):
    rows = slots[slot] if factor is None else slots[slot] * factor
    o_ref[slot * 8 : slot * 8 + 8, first : first + BUCKET, :] = (
        rows.astype(jnp.bfloat16).reshape(8, BUCKET, HEAD_DIM)
    )


def put_prompt(o_ref, first, rows, factor=None):
    rows = rows[...] if factor is None else rows[...] * factor
    o_ref[:, first : first + PROWS, :] = rows.astype(jnp.bfloat16).reshape(HEADS, PROWS, HEAD_DIM)


def split_copies(source, target, sems, count):
    size = source.shape[0] // count
    return [
        pltpu.make_async_copy(
            source.at[pl.ds(part * size, size)], target.at[pl.ds(part * size, size)], sems.at[part]
        )
        for part in range(count)
    ]


def start_all(copies):
    for copy in copies:
        copy.start()


def wait_all(copies):
    for copy in copies:
        copy.wait()


def prob_kernel(
    len_ref, x_hbm, p_hbm, o_hbm, x_ref, stage, o_ref, s_ref, e_ref, acc_p, acc_c, top_ref, inv_ref,
    in_sems, p_sems, o_sems
):
    load = split_copies(x_hbm, x_ref, in_sems, PARTS)
    start_all(load)
    blocks = live_blocks(len_ref)
    for ref in (acc_p, acc_c):
        ref[...] = jnp.zeros_like(ref)
    wait_all(load)

    def save(index):
        slot = lax.rem(index, 2)
        return split_copies(stage.at[slot], p_hbm.at[index], p_sems.at[slot], PARTS)

    def run(step, score, exponent, weigh):
        slot, place = locate(len_ref, step)
        old_slot, old_place = locate(len_ref, step - 2)
        old = lax.rem(step, 2)
        length = len_ref[slot]
        queries = rows_of(x_ref, slot * 8 + place * (QB // BUCKET), QB // BUCKET, Q0, Q0 + BUCKET)
        grad_out = rows_of(
            x_ref, old_slot * 8 + old_place * (QB // BUCKET), QB // BUCKET, D0, D0 + BUCKET
        )
        top = top_ref[0:1, :]
        inverse = inv_ref[0:1, :]

        def body(rows, acc_rows, keys, low, carry):
            peak, total = carry
            if weigh:
                prob = (e_ref[rows, :] * inverse).astype(jnp.bfloat16)
                stage[old, rows, :] = prob
                grad = dot(prob, grad_out, NN)
                if low is None:
                    acc_p[acc_rows, :] += grad
                else:
                    acc_c[old_slot, acc_rows, :] += grad
            if exponent:
                expo = jnp.exp2(s_ref[rows, :] - top)
                e_ref[rows, :] = expo
                total = total + fold(expo, jnp.sum)
            if score:
                scores = dot(keys, queries, NT) * (TEMPER * LOG2E)
                if low is not None:
                    parts = []
                    for part in range(0, CHUNK, BUCKET):
                        seen = low + part < length
                        parts.append(jnp.where(seen, scores[part : part + BUCKET], HIDDEN))
                    scores = jnp.concatenate(parts, axis=0)
                s_ref[rows, :] = scores
                peak = jnp.maximum(peak, fold(scores, jnp.max))
            return peak, total

        peak, total = over_chunks(
            body,
            (jnp.full((FOLD, QB), HIDDEN, jnp.float32), jnp.zeros((FOLD, QB), jnp.float32)),
            lambda first, count: rows_of(x_ref, first, count, K0, K0 + BUCKET),
            lambda first, count: rows_of(x_ref, first, count, KP0, KP0 + PROWS),
            slot,
        )
        if score:
            top_ref[0:1, :] = jnp.max(peak, axis=0, keepdims=True)
        if exponent:
            inv_ref[0:1, :] = 1.0 / jnp.sum(total, axis=0, keepdims=True)

    run(0, True, False, False)
    run(1, True, True, False)

    @pl.loop(2, blocks)
    def _(step):
        @pl.when(step >= 4)
        def _():
            wait_all(save(step - 4))

        run(step, True, True, True)
        start_all(save(step - 2))

    wait_all(save(blocks - 4))
    run(blocks, False, True, True)
    start_all(save(blocks - 2))
    wait_all(save(blocks - 3))
    run(blocks + 1, False, False, True)
    start_all(save(blocks - 1))
    put_prompt(o_ref, DVP0, acc_p)
    store = split_copies(o_ref, o_hbm, o_sems, COMP)
    for slot in range(COMP):
        put_blocks(o_ref, DV0, acc_c, slot)
        store[slot].start()
    wait_all(save(blocks - 2))
    wait_all(save(blocks - 1))
    wait_all(store)


def score_kernel(
    len_ref, x_hbm, y_hbm, p_hbm, o_hbm, x_ref, y_ref, p_ref, o_ref, d_ref, acc_p, acc_c, dq_ref,
    kpt_ref, kct_ref, delta_ref, x_sems, y_sems, p_sems, o_sems
):
    load_x = split_copies(x_hbm, x_ref, x_sems, PARTS)
    load_y = split_copies(y_hbm, y_ref, y_sems, PARTS)
    start_all(load_x)

    def fetch(index):
        slot = lax.rem(index, 3)
        return split_copies(p_hbm.at[index], p_ref.at[slot], p_sems.at[slot], PARTS)

    start_all(load_y)
    start_all(fetch(0))
    start_all(fetch(1))
    blocks = live_blocks(len_ref)
    o_ref[:, DQ0 : DQ0 + BUCKET, :] = jnp.zeros((HEADS, BUCKET, HEAD_DIM), jnp.bfloat16)
    for ref in (acc_p, acc_c):
        ref[...] = jnp.zeros_like(ref)
    wait_all(load_x)
    kpt_ref[...] = rows_of(x_ref, 0, HEADS, KP0, KP0 + PROWS).T
    for slot in range(COMP):
        kct_ref[slot] = rows_of(x_ref, slot * 8, 8, K0, K0 + BUCKET).T
    wait_all(load_y)

    def run(step, probe, spread):
        slot, place = locate(len_ref, step)
        old_slot, old_place = locate(len_ref, step - 1)
        now = lax.rem(step, 3)
        old = lax.rem(step + 2, 3)
        grad_out = rows_of(x_ref, slot * 8 + place * (QB // BUCKET), QB // BUCKET, D0, D0 + BUCKET)
        old_first = old_slot * 8 + old_place * (QB // BUCKET)
        queries = rows_of(x_ref, old_first, QB // BUCKET, Q0, Q0 + BUCKET)
        delta = delta_ref[0:1, :]
        if spread:
            dq_ref[...] = jnp.zeros_like(dq_ref)

        def body(rows, acc_rows, values, low, partial):
            if spread:
                grad_s = (
                    p_ref[old, rows, :].astype(jnp.float32) * (d_ref[rows, :] - delta)
                ).astype(jnp.bfloat16)
                grad = dot(grad_s, queries, NN)
                if low is None:
                    acc_p[acc_rows, :] += grad
                    dq_ref[...] += dot(kpt_ref[:, acc_rows], grad_s, NN)
                else:
                    acc_c[old_slot, acc_rows, :] += grad
                    dq_ref[...] += dot(kct_ref[old_slot, :, acc_rows], grad_s, NN)
            if probe:
                grad_prob = dot(values, grad_out, NT)
                d_ref[rows, :] = grad_prob
                partial = partial + fold(p_ref[now, rows, :].astype(jnp.float32) * grad_prob, jnp.sum)
            return partial

        partial = over_chunks(
            body,
            jnp.zeros((FOLD, QB), jnp.float32),
            lambda first, count: rows_of(y_ref, first, count, V0, V0 + BUCKET),
            lambda first, count: rows_of(y_ref, first, count, VP0, VP0 + PROWS),
            slot,
        )
        if probe:
            delta_ref[0:1, :] = jnp.sum(partial, axis=0, keepdims=True)
        if spread:
            o_ref[pl.ds(old_first, QB // BUCKET), DQ0 : DQ0 + BUCKET, :] = (
                (dq_ref[...].T * TEMPER).astype(jnp.bfloat16).reshape(QB // BUCKET, BUCKET, HEAD_DIM)
            )

    wait_all(fetch(0))
    run(0, True, False)

    @pl.loop(1, blocks)
    def _(step):
        @pl.when(step + 1 < blocks)
        def _():
            start_all(fetch(step + 1))

        wait_all(fetch(step))
        run(step, True, True)

    run(blocks, False, True)
    put_prompt(o_ref, DKP0, acc_p, TEMPER)
    store = split_copies(o_ref, o_hbm, o_sems, COMP)
    for slot in range(COMP):
        put_blocks(o_ref, DK0, acc_c, slot, TEMPER)
        store[slot].start()
    wait_all(store)


MAX_BLOCKS = COMP * QSTEPS
PRODUCT = 2 * COMP * LMAX * KEYS * HEAD_DIM
FAR = pl.BlockSpec(memory_space=pltpu.HBM)
SCALARS = pl.BlockSpec(memory_space=pltpu.SMEM)


def sems(*shape):
    return pltpu.SemaphoreType.DMA(shape)


def blocks_of(rows):
    return (HEADS, rows, HEAD_DIM)


def run_prob(lengths, first):
    return pl.pallas_call(
        prob_kernel,
        in_specs=[SCALARS, FAR],
        out_specs=[FAR, FAR],
        scratch_shapes=[
            pltpu.VMEM(blocks_of(ROWS1), jnp.bfloat16),
            pltpu.VMEM((2, KEYS, QB), jnp.bfloat16),
            pltpu.VMEM(blocks_of(ROWS3), jnp.bfloat16),
            pltpu.VMEM((KEYS, QB), jnp.float32),
            pltpu.VMEM((KEYS, QB), jnp.float32),
            pltpu.VMEM((PROMPT, HEAD_DIM), jnp.float32),
            pltpu.VMEM((COMP, LMAX, HEAD_DIM), jnp.float32),
            pltpu.VMEM((8, QB), jnp.float32),
            pltpu.VMEM((8, QB), jnp.float32),
            sems(PARTS),
            sems(2, PARTS),
            sems(PARTS),
        ],
        out_shape=[
            jax.ShapeDtypeStruct((MAX_BLOCKS, KEYS, QB), jnp.bfloat16),
            jax.ShapeDtypeStruct(blocks_of(ROWS3), jnp.bfloat16),
        ],
        compiler_params=pltpu.CompilerParams(vmem_limit_bytes=VMEM_LIMIT),
        cost_estimate=pl.CostEstimate(
            flops=2 * PRODUCT, bytes_accessed=30 * 2**20, transcendentals=COMP * LMAX * KEYS
        ),
        name="attn_prob",
    )(lengths, first)


def run_score(lengths, first, second, prob):
    return pl.pallas_call(
        score_kernel,
        in_specs=[SCALARS, FAR, FAR, FAR],
        out_specs=FAR,
        scratch_shapes=[
            pltpu.VMEM(blocks_of(ROWS1), jnp.bfloat16),
            pltpu.VMEM(blocks_of(ROWS2), jnp.bfloat16),
            pltpu.VMEM((3, KEYS, QB), jnp.bfloat16),
            pltpu.VMEM(blocks_of(ROWS4), jnp.bfloat16),
            pltpu.VMEM((KEYS, QB), jnp.float32),
            pltpu.VMEM((PROMPT, HEAD_DIM), jnp.float32),
            pltpu.VMEM((COMP, LMAX, HEAD_DIM), jnp.float32),
            pltpu.VMEM((HEAD_DIM, QB), jnp.float32),
            pltpu.VMEM((HEAD_DIM, PROMPT), jnp.bfloat16),
            pltpu.VMEM((COMP, HEAD_DIM, LMAX), jnp.bfloat16),
            pltpu.VMEM((8, QB), jnp.float32),
            sems(PARTS),
            sems(PARTS),
            sems(3, PARTS),
            sems(PARTS),
        ],
        out_shape=jax.ShapeDtypeStruct(blocks_of(ROWS4), jnp.bfloat16),
        compiler_params=pltpu.CompilerParams(vmem_limit_bytes=VMEM_LIMIT),
        cost_estimate=pl.CostEstimate(
            flops=3 * PRODUCT, bytes_accessed=30 * 2**20, transcendentals=0
        ),
        name="grad_scores",
    )(lengths, first, second, prob)


WIDE = 8


def pack_kernel(
    len_hbm, gain_hbm, mask_hbm, q_hbm, k_hbm, c_hbm, kp_hbm, o_hbm,
    len_ref, gain_ref, mask_ref, q_ref, k_ref, c_ref, kp_ref, o_ref, factor_ref,
    few_sems, in_sems, out_sems
):
    few = [
        pltpu.make_async_copy(source, target, few_sems.at[index])
        for index, (source, target) in enumerate(
            ((len_hbm, len_ref), (gain_hbm, gain_ref), (mask_hbm, mask_ref))
        )
    ]
    start_all(few)
    width = WIDE * HEAD_DIM
    pairs = ((q_hbm, q_ref), (k_hbm, k_ref), (c_hbm, c_ref), (kp_hbm, kp_ref))
    loads, stores = [], []
    for part in range(HEADS // WIDE):
        lanes = pl.ds(part * width, width)
        loads.append(
            [
                pltpu.make_async_copy(
                    source.at[0, :, lanes], target.at[:, lanes], in_sems.at[part, index]
                )
                for index, (source, target) in enumerate(pairs)
            ]
        )
        heads = pl.ds(part * WIDE, WIDE)
        stores.append(pltpu.make_async_copy(o_ref.at[heads], o_hbm.at[heads], out_sems.at[part]))
        start_all(loads[-1])
    wait_all(few)
    me = lax.axis_index("seq")
    slot = lax.div(me, LMAX // BUCKET)
    place = (me - slot * (LMAX // BUCKET)) * BUCKET
    live = (mask_ref[...] * (place < len_ref[0, slot]).astype(jnp.int32)).astype(jnp.float32)
    factor_ref[...] = jnp.broadcast_to(live * gain_ref[0, slot], (HEAD_DIM, BUCKET)).T
    for part in range(HEADS // WIDE):
        wait_all(loads[part])
        for head in range(part * WIDE, part * WIDE + WIDE):
            lanes = slice(head * HEAD_DIM, head * HEAD_DIM + HEAD_DIM)
            o_ref[head, Q0 : Q0 + BUCKET, :] = q_ref[:, lanes]
            o_ref[head, K0 : K0 + BUCKET, :] = k_ref[:, lanes]
            o_ref[head, D0 : D0 + BUCKET, :] = (
                c_ref[:, lanes].astype(jnp.float32) * factor_ref[...]
            ).astype(jnp.bfloat16)
            o_ref[head, KP0 : KP0 + PROWS, :] = kp_ref[:, lanes]
        stores[part].start()
    wait_all(stores)


def wide_rows(rows):
    return pl.BlockSpec((1, rows, WIDE * HEAD_DIM), lambda step, *_: (0, 0, step))


def wide_heads(rows):
    return pl.BlockSpec((WIDE, rows, HEAD_DIM), lambda step, *_: (step, 0, 0))


def run_pack(lengths, gain, mask, queries, keys, cotangent, prompt_keys):
    wide = HEADS * HEAD_DIM
    return pl.pallas_call(
        pack_kernel,
        in_specs=[FAR] * 7,
        out_specs=FAR,
        scratch_shapes=[
            pltpu.SMEM((1, COMP), jnp.int32),
            pltpu.SMEM((1, COMP), jnp.float32),
            pltpu.VMEM((1, BUCKET), jnp.int32),
            pltpu.VMEM((BUCKET, wide), jnp.bfloat16),
            pltpu.VMEM((BUCKET, wide), jnp.bfloat16),
            pltpu.VMEM((BUCKET, wide), jnp.bfloat16),
            pltpu.VMEM((PROWS, wide), jnp.bfloat16),
            pltpu.VMEM(blocks_of(ROWS1), jnp.bfloat16),
            pltpu.VMEM((BUCKET, HEAD_DIM), jnp.float32),
            sems(3),
            sems(HEADS // WIDE, 4),
            sems(HEADS // WIDE),
        ],
        out_shape=jax.ShapeDtypeStruct(blocks_of(ROWS1), jnp.bfloat16),
        compiler_params=pltpu.CompilerParams(vmem_limit_bytes=VMEM_LIMIT),
        name="pack_first",
    )(lengths, gain, mask, queries, keys, cotangent, prompt_keys)


def run_unpack(name, blocks, scale, parts, limit):
    def kernel(scale_ref, x_ref, *o_refs):
        for head in range(WIDE):
            lanes = slice(head * HEAD_DIM, head * HEAD_DIM + HEAD_DIM)
            for (low, rows), o_ref in zip(parts, o_refs):
                o_ref[0, :, lanes] = (
                    x_ref[head, low : low + rows, :].astype(jnp.float32) * scale_ref[0]
                ).astype(jnp.bfloat16)

    return pl.pallas_call(
        kernel,
        grid_spec=pltpu.PrefetchScalarGridSpec(
            num_scalar_prefetch=1,
            grid=(HEADS // WIDE,),
            in_specs=[wide_heads(blocks.shape[1])],
            out_specs=[wide_rows(rows) for _, rows in parts],
        ),
        out_shape=[
            jax.ShapeDtypeStruct((1, rows, HEADS * HEAD_DIM), jnp.bfloat16) for _, rows in parts
        ],
        compiler_params=pltpu.CompilerParams(
            dimension_semantics=("arbitrary",), vmem_limit_bytes=limit
        ),
        name=name,
    )(scale, blocks)


def to_heads(matrix):
    return matrix.reshape(matrix.shape[0], HEADS, HEAD_DIM).transpose(1, 0, 2)


def exchange(blocks):
    return lax.all_to_all(blocks, "seq", split_axis=0, concat_axis=0, tiled=True)


def on_device(comp_q, comp_k, comp_v, cotangent, prompt_k, prompt_v, lengths, loss_mask, advantage):
    row_count = comp_q.shape[1]
    seq_ways = lax.axis_size("seq")
    grp_ways = lax.axis_size("grp")
    slot_total = lengths.shape[1]
    token_ids = lax.axis_index("seq") * row_count + jnp.arange(row_count, dtype=jnp.int32)
    slot_ids = token_ids // LMAX
    position = token_ids % LMAX
    member = slot_ids[:, None] == jnp.arange(slot_total, dtype=jnp.int32)[None, :]
    token_limit = jnp.sum(jnp.where(member, lengths[0][None, :], 0), axis=1)
    live_weight = (loss_mask[0] * (position < token_limit).astype(jnp.int32)).astype(jnp.float32)
    count = jnp.broadcast_to(
        jnp.sum(live_weight).astype(jnp.bfloat16), (HEADS, ROWS2 - CNT0, HEAD_DIM)
    )
    send_first = run_pack(
        lengths, advantage, loss_mask, comp_q, comp_k, cotangent, prompt_k
    )
    first = exchange(send_first)
    send_second = jnp.concatenate([to_heads(comp_v[0]), to_heads(prompt_v[0]), count], axis=1)
    send_second, first = lax.optimization_barrier((send_second, first))
    second = exchange(send_second)
    prob, send_third = run_prob(lengths[0], first)
    live_total = jnp.sum(second[:, CNT0, 0].astype(jnp.float32)).reshape(1, 1)
    send_third, second = lax.optimization_barrier((send_third, second))
    third = exchange(send_third)
    for other in (1, 2):
        live_total = live_total + lax.ppermute(
            live_total, "grp", [(index, index ^ other) for index in range(grp_ways)]
        )
    loss_scale = grp_ways * seq_ways * row_count / jnp.maximum(live_total[0, 0], 1.0)
    send_fourth = run_score(lengths[0], first, second, prob)
    send_fourth, third = lax.optimization_barrier((send_fourth, third))
    fourth = exchange(send_fourth)

    loss_scale = loss_scale.astype(jnp.float32).reshape(1)
    grad_v, grad_vp = run_unpack("unpack_third", third, loss_scale, ((DV0, BUCKET), (DVP0, PROWS)), VMEM_LIMIT)
    grad_k, grad_q, grad_kp = run_unpack(
        "unpack_fourth", fourth, loss_scale, ((DK0, BUCKET), (DQ0, BUCKET), (DKP0, PROWS)), 16 * 2**20
    )
    return grad_q, grad_k, grad_v, grad_kp, grad_vp


def solution(mesh):
    return jax.shard_map(
        on_device,
        mesh=mesh,
        in_specs=(
            P("grp", "seq", None),
            P("grp", "seq", None),
            P("grp", "seq", None),
            P("grp", "seq", None),
            P("grp", "seq", None),
            P("grp", "seq", None),
            P("grp", None),
            P("grp", "seq"),
            P("grp", None),
        ),
        out_specs=(
            P("grp", "seq", None),
            P("grp", "seq", None),
            P("grp", "seq", None),
            P("grp", "seq", None),
            P("grp", "seq", None),
        ),
        check_vma=False,
    )
```

```python
import jax
import jax.numpy as jnp
from jax import lax
from jax.experimental import pallas as pl
from jax.experimental.pallas import tpu as pltpu
from jax.sharding import PartitionSpec as P

HEADS = 32
HEAD_DIM = 128
LMAX = 1024
PROMPT = 2048
COMP = 4
BUCKET = 128
PROWS = 64
KEYS = PROMPT + LMAX
QB = 256
QSTEPS = LMAX // QB
CHUNK = 1024
FOLD = 16
VMEM_LIMIT = 63 * 2**20
PARTS = 2
TEMPER = HEAD_DIM ** (-0.5)
LOG2E = 1.4426950408889634
HIDDEN = -1e30

Q0, K0, D0, KP0, ROWS1 = 0, 128, 256, 384, 448
V0, VP0, CNT0, ROWS2 = 0, 128, 192, 200
DV0, DVP0, ROWS3 = 0, 128, 192
DK0, DQ0, DKP0, ROWS4 = 0, 128, 256, 320

NT = (((1,), (1,)), ((), ()))
NN = (((1,), (0,)), ((), ()))


def dot(left, right, dims):
    return lax.dot_general(left, right, dims, preferred_element_type=jnp.float32)


def rows_of(ref, first, count, low, high):
    return ref[pl.ds(first, count), low:high, :].reshape(count * (high - low), HEAD_DIM)


def fold(values, op):
    return op(values.reshape(values.shape[0] // FOLD, FOLD, values.shape[1]), axis=0)


def block_counts(lens):
    return [lax.div(lens[slot] + (QB - 1), QB) for slot in range(COMP)]


def locate(lens, index):
    counts = block_counts(lens)
    ends, end = [], 0
    for count in counts:
        end = end + count
        ends.append(end)
    index = jnp.clip(index, 0, end - 1)
    slot, base = 0, 0
    for place in range(COMP - 1):
        passed = index >= ends[place]
        slot = slot + passed.astype(jnp.int32)
        base = jnp.where(passed, ends[place], base)
    return slot, index - base


def live_blocks(lens):
    return sum(block_counts(lens))


def over_chunks(body, carry, comp_rows, prompt_rows, slot):
    per_prompt, per_comp = CHUNK // PROWS, CHUNK // BUCKET

    for low in range(0, PROMPT, CHUNK):
        rows = slice(low, low + CHUNK)
        carry = body(rows, rows, prompt_rows(low // PROWS, per_prompt), None, carry)
    for low in range(0, LMAX, CHUNK):
        rows = slice(PROMPT + low, PROMPT + low + CHUNK)
        acc_rows = slice(low, low + CHUNK)
        carry = body(rows, acc_rows, comp_rows(slot * 8 + low // BUCKET, per_comp), low, carry)
    return carry


def put_blocks(o_ref, first, slots, slot, factor=None):
    rows = slots[slot] if factor is None else slots[slot] * factor
    o_ref[pl.ds(slot * 8, 8), first : first + BUCKET, :] = (
        rows.astype(jnp.bfloat16).reshape(8, BUCKET, HEAD_DIM)
    )


def put_prompt(o_ref, first, rows, factor=None):
    rows = rows[...] if factor is None else rows[...] * factor
    o_ref[:, first : first + PROWS, :] = rows.astype(jnp.bfloat16).reshape(HEADS, PROWS, HEAD_DIM)


def split_copies(source, target, sems, count):
    size = source.shape[0] // count
    return [
        pltpu.make_async_copy(
            source.at[pl.ds(part * size, size)], target.at[pl.ds(part * size, size)], sems.at[part]
        )
        for part in range(count)
    ]


def start_all(copies):
    for copy in copies:
        copy.start()


def wait_all(copies):
    for copy in copies:
        copy.wait()


class Loads:
    def __init__(self, source, target, sems, low, high):
        self.source, self.target, self.sems, self.low, self.high = source, target, sems, low, high

    def copy(self, index, *place):
        return pltpu.make_async_copy(
            self.source.at[place], self.target.at[place], self.sems.at[index]
        )

    def prompt(self):
        return self.copy(COMP, slice(None), pl.ds(self.low, self.high - self.low))

    def slot(self, slot):
        first = slot * 8 if isinstance(slot, int) else pl.multiple_of(slot * 8, 8)
        return self.copy(slot, pl.ds(first, 8), pl.ds(0, self.low))

    def start(self):
        self.prompt().start()
        for slot in range(COMP):
            self.slot(slot).start()


def prob_kernel(
    len_ref, x_hbm, p_hbm, o_hbm, x_ref, stage, o_ref, s_ref, e_ref, acc_p, acc_c, top_ref, inv_ref,
    in_sems, p_sems, o_sems
):
    load = Loads(x_hbm, x_ref, in_sems, KP0, ROWS1)
    load.start()
    blocks = live_blocks(len_ref)
    for ref in (acc_p, acc_c):
        ref[...] = jnp.zeros_like(ref)
    load.prompt().wait()
    load.slot(0).wait()
    store = Loads(o_ref, o_hbm, o_sems, DVP0, ROWS3)

    def save(index):
        slot = lax.rem(index, 2)
        return split_copies(stage.at[slot], p_hbm.at[index], p_sems.at[slot], PARTS)

    def run(step, score, exponent, weigh):
        slot, place = locate(len_ref, step)
        old_slot, old_place = locate(len_ref, step - 2)
        old = lax.rem(step, 2)
        length = len_ref[slot]
        queries = rows_of(x_ref, slot * 8 + place * (QB // BUCKET), QB // BUCKET, Q0, Q0 + BUCKET)
        grad_out = rows_of(
            x_ref, old_slot * 8 + old_place * (QB // BUCKET), QB // BUCKET, D0, D0 + BUCKET
        )
        top = top_ref[0:1, :]
        inverse = inv_ref[0:1, :]

        def body(rows, acc_rows, keys, low, carry):
            peak, total = carry
            if weigh:
                prob = (e_ref[rows, :] * inverse).astype(jnp.bfloat16)
                stage[old, rows, :] = prob
                grad = dot(prob, grad_out, NN)
                if low is None:
                    acc_p[acc_rows, :] += grad
                else:
                    acc_c[old_slot, acc_rows, :] += grad
            if exponent:
                expo = jnp.exp2(s_ref[rows, :] - top)
                e_ref[rows, :] = expo
                total = total + fold(expo, jnp.sum)
            if score:
                scores = dot(keys, queries, NT) * (TEMPER * LOG2E)
                if low is not None:
                    parts = []
                    for part in range(0, CHUNK, BUCKET):
                        seen = low + part < length
                        parts.append(jnp.where(seen, scores[part : part + BUCKET], HIDDEN))
                    scores = jnp.concatenate(parts, axis=0)
                s_ref[rows, :] = scores
                peak = jnp.maximum(peak, fold(scores, jnp.max))
            return peak, total

        peak, total = over_chunks(
            body,
            (jnp.full((FOLD, QB), HIDDEN, jnp.float32), jnp.zeros((FOLD, QB), jnp.float32)),
            lambda first, count: rows_of(x_ref, first, count, K0, K0 + BUCKET),
            lambda first, count: rows_of(x_ref, first, count, KP0, KP0 + PROWS),
            slot,
        )
        if score:
            top_ref[0:1, :] = jnp.max(peak, axis=0, keepdims=True)
        if exponent:
            inv_ref[0:1, :] = 1.0 / jnp.sum(total, axis=0, keepdims=True)

    def enter(step):
        slot, place = locate(len_ref, step)

        @pl.when((slot > 0) & (place == 0))
        def _():
            load.slot(slot).wait()

    def leave(step):
        slot, place = locate(len_ref, step - 2)

        @pl.when((slot > 0) & (place == 0))
        def _():
            put_blocks(o_ref, DV0, acc_c, slot - 1)
            store.slot(slot - 1).start()

    run(0, True, False, False)
    enter(1)
    run(1, True, True, False)

    @pl.loop(2, blocks)
    def _(step):
        @pl.when(step >= 4)
        def _():
            wait_all(save(step - 4))

        enter(step)
        leave(step)
        run(step, True, True, True)
        start_all(save(step - 2))

    wait_all(save(blocks - 4))
    leave(blocks)
    run(blocks, False, True, True)
    start_all(save(blocks - 2))
    wait_all(save(blocks - 3))
    leave(blocks + 1)
    run(blocks + 1, False, False, True)
    start_all(save(blocks - 1))
    put_blocks(o_ref, DV0, acc_c, COMP - 1)
    store.slot(COMP - 1).start()
    put_prompt(o_ref, DVP0, acc_p)
    store.prompt().start()
    wait_all(save(blocks - 2))
    wait_all(save(blocks - 1))
    store.prompt().wait()
    for slot in range(COMP):
        store.slot(slot).wait()


def score_kernel(
    len_ref, x_hbm, y_hbm, p_hbm, o_hbm, x_ref, y_ref, p_ref, o_ref, d_ref, acc_p, acc_c, dq_ref,
    kpt_ref, kct_ref, delta_ref, x_sems, y_sems, p_sems, o_sems
):
    load_x = Loads(x_hbm, x_ref, x_sems, KP0, ROWS1)
    load_y = Loads(y_hbm, y_ref, y_sems, VP0, ROWS2)
    store = Loads(o_ref, o_hbm, o_sems, DKP0, ROWS4)

    def fetch(index):
        slot = lax.rem(index, 3)
        return split_copies(p_hbm.at[index], p_ref.at[slot], p_sems.at[slot], PARTS)

    load_y.prompt().start()
    load_y.slot(0).start()
    load_x.slot(0).start()
    start_all(fetch(0))
    load_x.prompt().start()
    for slot in range(1, COMP):
        load_y.slot(slot).start()
        load_x.slot(slot).start()
    start_all(fetch(1))
    blocks = live_blocks(len_ref)
    o_ref[:, DQ0 : DQ0 + BUCKET, :] = jnp.zeros((HEADS, BUCKET, HEAD_DIM), jnp.bfloat16)
    for ref in (acc_p, acc_c):
        ref[...] = jnp.zeros_like(ref)
    load_y.prompt().wait()

    def admit(slot):
        load_y.slot(slot).wait()
        load_x.slot(slot).wait()
        kct_ref[slot] = rows_of(x_ref, slot * 8, 8, K0, K0 + BUCKET).T

    def enter(step):
        slot, place = locate(len_ref, step)

        @pl.when((slot > 0) & (place == 0))
        def _():
            admit(slot)

    def leave(step):
        slot, place = locate(len_ref, step - 1)

        @pl.when((slot > 0) & (place == 0))
        def _():
            put_blocks(o_ref, DK0, acc_c, slot - 1, TEMPER)
            store.slot(slot - 1).start()

    def run(step, probe, spread):
        slot, place = locate(len_ref, step)
        old_slot, old_place = locate(len_ref, step - 1)
        now = lax.rem(step, 3)
        old = lax.rem(step + 2, 3)
        grad_out = rows_of(x_ref, slot * 8 + place * (QB // BUCKET), QB // BUCKET, D0, D0 + BUCKET)
        old_first = old_slot * 8 + old_place * (QB // BUCKET)
        queries = rows_of(x_ref, old_first, QB // BUCKET, Q0, Q0 + BUCKET)
        delta = delta_ref[0:1, :]
        if spread:
            dq_ref[...] = jnp.zeros_like(dq_ref)

        def body(rows, acc_rows, values, low, partial):
            if spread:
                grad_s = (
                    p_ref[old, rows, :].astype(jnp.float32) * (d_ref[rows, :] - delta)
                ).astype(jnp.bfloat16)
                grad = dot(grad_s, queries, NN)
                if low is None:
                    acc_p[acc_rows, :] += grad
                    dq_ref[...] += dot(kpt_ref[:, acc_rows], grad_s, NN)
                else:
                    acc_c[old_slot, acc_rows, :] += grad
                    dq_ref[...] += dot(kct_ref[old_slot, :, acc_rows], grad_s, NN)
            if probe:
                grad_prob = dot(values, grad_out, NT)
                d_ref[rows, :] = grad_prob
                partial = partial + fold(p_ref[now, rows, :].astype(jnp.float32) * grad_prob, jnp.sum)
            return partial

        partial = over_chunks(
            body,
            jnp.zeros((FOLD, QB), jnp.float32),
            lambda first, count: rows_of(y_ref, first, count, V0, V0 + BUCKET),
            lambda first, count: rows_of(y_ref, first, count, VP0, VP0 + PROWS),
            slot,
        )
        if probe:
            delta_ref[0:1, :] = jnp.sum(partial, axis=0, keepdims=True)
        if spread:
            o_ref[pl.ds(old_first, QB // BUCKET), DQ0 : DQ0 + BUCKET, :] = (
                (dq_ref[...].T * TEMPER).astype(jnp.bfloat16).reshape(QB // BUCKET, BUCKET, HEAD_DIM)
            )

    admit(0)
    wait_all(fetch(0))
    run(0, True, False)
    load_x.prompt().wait()
    kpt_ref[...] = rows_of(x_ref, 0, HEADS, KP0, KP0 + PROWS).T

    @pl.loop(1, blocks)
    def _(step):
        @pl.when(step + 1 < blocks)
        def _():
            start_all(fetch(step + 1))

        enter(step)
        leave(step)
        wait_all(fetch(step))
        run(step, True, True)

    leave(blocks)
    run(blocks, False, True)
    put_blocks(o_ref, DK0, acc_c, COMP - 1, TEMPER)
    store.slot(COMP - 1).start()
    put_prompt(o_ref, DKP0, acc_p, TEMPER)
    store.prompt().start()
    store.prompt().wait()
    for slot in range(COMP):
        store.slot(slot).wait()


MAX_BLOCKS = COMP * QSTEPS
PRODUCT = 2 * COMP * LMAX * KEYS * HEAD_DIM
FAR = pl.BlockSpec(memory_space=pltpu.HBM)
SCALARS = pl.BlockSpec(memory_space=pltpu.SMEM)


def sems(*shape):
    return pltpu.SemaphoreType.DMA(shape)


def blocks_of(rows):
    return (HEADS, rows, HEAD_DIM)


def run_prob(lengths, first):
    return pl.pallas_call(
        prob_kernel,
        in_specs=[SCALARS, FAR],
        out_specs=[FAR, FAR],
        scratch_shapes=[
            pltpu.VMEM(blocks_of(ROWS1), jnp.bfloat16),
            pltpu.VMEM((2, KEYS, QB), jnp.bfloat16),
            pltpu.VMEM(blocks_of(ROWS3), jnp.bfloat16),
            pltpu.VMEM((KEYS, QB), jnp.float32),
            pltpu.VMEM((KEYS, QB), jnp.float32),
            pltpu.VMEM((PROMPT, HEAD_DIM), jnp.float32),
            pltpu.VMEM((COMP, LMAX, HEAD_DIM), jnp.float32),
            pltpu.VMEM((8, QB), jnp.float32),
            pltpu.VMEM((8, QB), jnp.float32),
            sems(COMP + 1),
            sems(2, PARTS),
            sems(COMP + 1),
        ],
        out_shape=[
            jax.ShapeDtypeStruct((MAX_BLOCKS, KEYS, QB), jnp.bfloat16),
            jax.ShapeDtypeStruct(blocks_of(ROWS3), jnp.bfloat16),
        ],
        compiler_params=pltpu.CompilerParams(vmem_limit_bytes=VMEM_LIMIT),
        cost_estimate=pl.CostEstimate(
            flops=2 * PRODUCT, bytes_accessed=30 * 2**20, transcendentals=COMP * LMAX * KEYS
        ),
        name="attn_prob",
    )(lengths, first)


def run_score(lengths, first, second, prob):
    return pl.pallas_call(
        score_kernel,
        in_specs=[SCALARS, FAR, FAR, FAR],
        out_specs=FAR,
        scratch_shapes=[
            pltpu.VMEM(blocks_of(ROWS1), jnp.bfloat16),
            pltpu.VMEM(blocks_of(ROWS2), jnp.bfloat16),
            pltpu.VMEM((3, KEYS, QB), jnp.bfloat16),
            pltpu.VMEM(blocks_of(ROWS4), jnp.bfloat16),
            pltpu.VMEM((KEYS, QB), jnp.float32),
            pltpu.VMEM((PROMPT, HEAD_DIM), jnp.float32),
            pltpu.VMEM((COMP, LMAX, HEAD_DIM), jnp.float32),
            pltpu.VMEM((HEAD_DIM, QB), jnp.float32),
            pltpu.VMEM((HEAD_DIM, PROMPT), jnp.bfloat16),
            pltpu.VMEM((COMP, HEAD_DIM, LMAX), jnp.bfloat16),
            pltpu.VMEM((8, QB), jnp.float32),
            sems(COMP + 1),
            sems(COMP + 1),
            sems(3, PARTS),
            sems(COMP + 1),
        ],
        out_shape=jax.ShapeDtypeStruct(blocks_of(ROWS4), jnp.bfloat16),
        compiler_params=pltpu.CompilerParams(vmem_limit_bytes=VMEM_LIMIT),
        cost_estimate=pl.CostEstimate(
            flops=3 * PRODUCT, bytes_accessed=30 * 2**20, transcendentals=0
        ),
        name="grad_scores",
    )(lengths, first, second, prob)


WIDE = 8


def pack_kernel(
    len_hbm, gain_hbm, mask_hbm, q_hbm, k_hbm, c_hbm, kp_hbm, o_hbm,
    len_ref, gain_ref, mask_ref, q_ref, k_ref, c_ref, kp_ref, o_ref, factor_ref,
    few_sems, in_sems, out_sems
):
    few = [
        pltpu.make_async_copy(source, target, few_sems.at[index])
        for index, (source, target) in enumerate(
            ((len_hbm, len_ref), (gain_hbm, gain_ref), (mask_hbm, mask_ref))
        )
    ]
    start_all(few)
    width = WIDE * HEAD_DIM
    pairs = ((q_hbm, q_ref), (k_hbm, k_ref), (c_hbm, c_ref), (kp_hbm, kp_ref))
    loads, stores = [], []
    for part in range(HEADS // WIDE):
        lanes = pl.ds(part * width, width)
        loads.append(
            [
                pltpu.make_async_copy(
                    source.at[0, :, lanes], target.at[:, lanes], in_sems.at[part, index]
                )
                for index, (source, target) in enumerate(pairs)
            ]
        )
        heads = pl.ds(part * WIDE, WIDE)
        stores.append(pltpu.make_async_copy(o_ref.at[heads], o_hbm.at[heads], out_sems.at[part]))
        start_all(loads[-1])
    wait_all(few)
    me = lax.axis_index("seq")
    slot = lax.div(me, LMAX // BUCKET)
    place = (me - slot * (LMAX // BUCKET)) * BUCKET
    live = (mask_ref[...] * (place < len_ref[0, slot]).astype(jnp.int32)).astype(jnp.float32)
    factor_ref[...] = jnp.broadcast_to(live * gain_ref[0, slot], (HEAD_DIM, BUCKET)).T
    for part in range(HEADS // WIDE):
        wait_all(loads[part])
        for head in range(part * WIDE, part * WIDE + WIDE):
            lanes = slice(head * HEAD_DIM, head * HEAD_DIM + HEAD_DIM)
            o_ref[head, Q0 : Q0 + BUCKET, :] = q_ref[:, lanes]
            o_ref[head, K0 : K0 + BUCKET, :] = k_ref[:, lanes]
            o_ref[head, D0 : D0 + BUCKET, :] = (
                c_ref[:, lanes].astype(jnp.float32) * factor_ref[...]
            ).astype(jnp.bfloat16)
            o_ref[head, KP0 : KP0 + PROWS, :] = kp_ref[:, lanes]
        stores[part].start()
    wait_all(stores)


def wide_rows(rows):
    return pl.BlockSpec((1, rows, WIDE * HEAD_DIM), lambda step, *_: (0, 0, step))


def wide_heads(rows):
    return pl.BlockSpec((WIDE, rows, HEAD_DIM), lambda step, *_: (step, 0, 0))


def run_pack(lengths, gain, mask, queries, keys, cotangent, prompt_keys):
    wide = HEADS * HEAD_DIM
    return pl.pallas_call(
        pack_kernel,
        in_specs=[FAR] * 7,
        out_specs=FAR,
        scratch_shapes=[
            pltpu.SMEM((1, COMP), jnp.int32),
            pltpu.SMEM((1, COMP), jnp.float32),
            pltpu.VMEM((1, BUCKET), jnp.int32),
            pltpu.VMEM((BUCKET, wide), jnp.bfloat16),
            pltpu.VMEM((BUCKET, wide), jnp.bfloat16),
            pltpu.VMEM((BUCKET, wide), jnp.bfloat16),
            pltpu.VMEM((PROWS, wide), jnp.bfloat16),
            pltpu.VMEM(blocks_of(ROWS1), jnp.bfloat16),
            pltpu.VMEM((BUCKET, HEAD_DIM), jnp.float32),
            sems(3),
            sems(HEADS // WIDE, 4),
            sems(HEADS // WIDE),
        ],
        out_shape=jax.ShapeDtypeStruct(blocks_of(ROWS1), jnp.bfloat16),
        compiler_params=pltpu.CompilerParams(vmem_limit_bytes=VMEM_LIMIT),
        name="pack_first",
    )(lengths, gain, mask, queries, keys, cotangent, prompt_keys)


def run_unpack(name, blocks, scale, parts, limit):
    def kernel(scale_ref, x_ref, *o_refs):
        for head in range(WIDE):
            lanes = slice(head * HEAD_DIM, head * HEAD_DIM + HEAD_DIM)
            for (low, rows), o_ref in zip(parts, o_refs):
                o_ref[0, :, lanes] = (
                    x_ref[head, low : low + rows, :].astype(jnp.float32) * scale_ref[0]
                ).astype(jnp.bfloat16)

    return pl.pallas_call(
        kernel,
        grid_spec=pltpu.PrefetchScalarGridSpec(
            num_scalar_prefetch=1,
            grid=(HEADS // WIDE,),
            in_specs=[wide_heads(blocks.shape[1])],
            out_specs=[wide_rows(rows) for _, rows in parts],
        ),
        out_shape=[
            jax.ShapeDtypeStruct((1, rows, HEADS * HEAD_DIM), jnp.bfloat16) for _, rows in parts
        ],
        compiler_params=pltpu.CompilerParams(
            dimension_semantics=("arbitrary",), vmem_limit_bytes=limit
        ),
        name=name,
    )(scale, blocks)


def to_heads(matrix):
    return matrix.reshape(matrix.shape[0], HEADS, HEAD_DIM).transpose(1, 0, 2)


def exchange(blocks):
    return lax.all_to_all(blocks, "seq", split_axis=0, concat_axis=0, tiled=True)


def on_device(comp_q, comp_k, comp_v, cotangent, prompt_k, prompt_v, lengths, loss_mask, advantage):
    row_count = comp_q.shape[1]
    seq_ways = lax.axis_size("seq")
    grp_ways = lax.axis_size("grp")
    slot_total = lengths.shape[1]
    token_ids = lax.axis_index("seq") * row_count + jnp.arange(row_count, dtype=jnp.int32)
    slot_ids = token_ids // LMAX
    position = token_ids % LMAX
    member = slot_ids[:, None] == jnp.arange(slot_total, dtype=jnp.int32)[None, :]
    token_limit = jnp.sum(jnp.where(member, lengths[0][None, :], 0), axis=1)
    live_weight = (loss_mask[0] * (position < token_limit).astype(jnp.int32)).astype(jnp.float32)
    count = jnp.broadcast_to(
        jnp.sum(live_weight).astype(jnp.bfloat16), (HEADS, ROWS2 - CNT0, HEAD_DIM)
    )
    send_first = run_pack(
        lengths, advantage, loss_mask, comp_q, comp_k, cotangent, prompt_k
    )
    first = exchange(send_first)
    send_second = jnp.concatenate([to_heads(comp_v[0]), to_heads(prompt_v[0]), count], axis=1)
    send_second, first = lax.optimization_barrier((send_second, first))
    second = exchange(send_second)
    prob, send_third = run_prob(lengths[0], first)
    live_total = jnp.sum(second[:, CNT0, 0].astype(jnp.float32)).reshape(1, 1)
    send_third, second = lax.optimization_barrier((send_third, second))
    third = exchange(send_third)
    for other in (1, 2):
        live_total = live_total + lax.ppermute(
            live_total, "grp", [(index, index ^ other) for index in range(grp_ways)]
        )
    loss_scale = grp_ways * seq_ways * row_count / jnp.maximum(live_total[0, 0], 1.0)
    send_fourth = run_score(lengths[0], first, second, prob)
    send_fourth, third = lax.optimization_barrier((send_fourth, third))
    fourth = exchange(send_fourth)

    loss_scale = loss_scale.astype(jnp.float32).reshape(1)
    grad_v, grad_vp = run_unpack("unpack_third", third, loss_scale, ((DV0, BUCKET), (DVP0, PROWS)), 16 * 2**20)
    grad_k, grad_q, grad_kp = run_unpack(
        "unpack_fourth", fourth, loss_scale, ((DK0, BUCKET), (DQ0, BUCKET), (DKP0, PROWS)), 16 * 2**20
    )
    return grad_q, grad_k, grad_v, grad_kp, grad_vp


def solution(mesh):
    return jax.shard_map(
        on_device,
        mesh=mesh,
        in_specs=(
            P("grp", "seq", None),
            P("grp", "seq", None),
            P("grp", "seq", None),
            P("grp", "seq", None),
            P("grp", "seq", None),
            P("grp", "seq", None),
            P("grp", None),
            P("grp", "seq"),
            P("grp", None),
        ),
        out_specs=(
            P("grp", "seq", None),
            P("grp", "seq", None),
            P("grp", "seq", None),
            P("grp", "seq", None),
            P("grp", "seq", None),
        ),
        check_vma=False,
    )
```

```python
import jax
import jax.numpy as jnp
from jax import lax
from jax.experimental import pallas as pl
from jax.experimental.pallas import tpu as pltpu
from jax.sharding import PartitionSpec as P

HEADS = 32
HEAD_DIM = 128
LMAX = 1024
PROMPT = 2048
COMP = 4
BUCKET = 128
PROWS = 64
KEYS = PROMPT + LMAX
QB = 256
QSTEPS = LMAX // QB
CHUNK = 1024
FOLD = 16
VMEM_LIMIT = 63 * 2**20
PARTS = 2
TEMPER = HEAD_DIM ** (-0.5)
LOG2E = 1.4426950408889634
HIDDEN = -1e30

Q0, K0, D0, KP0, ROWS1 = 0, 128, 256, 384, 448
V0, VP0, CNT0, ROWS2 = 0, 128, 192, 200
DV0, DVP0, ROWS3 = 0, 128, 192
DK0, DQ0, DKP0, ROWS4 = 0, 128, 256, 320

NT = (((1,), (1,)), ((), ()))
NN = (((1,), (0,)), ((), ()))


def dot(left, right, dims):
    return lax.dot_general(left, right, dims, preferred_element_type=jnp.float32)


def rows_of(ref, first, count, low, high):
    return ref[pl.ds(first, count), low:high, :].reshape(count * (high - low), HEAD_DIM)


def fold(values, op):
    return op(values.reshape(values.shape[0] // FOLD, FOLD, values.shape[1]), axis=0)


def block_counts(lens):
    return [lax.div(lens[slot] + (QB - 1), QB) for slot in range(COMP)]


def locate(lens, index):
    counts = block_counts(lens)
    ends, end = [], 0
    for count in counts:
        end = end + count
        ends.append(end)
    index = jnp.clip(index, 0, end - 1)
    slot, base = 0, 0
    for place in range(COMP - 1):
        passed = index >= ends[place]
        slot = slot + passed.astype(jnp.int32)
        base = jnp.where(passed, ends[place], base)
    return slot, index - base


def live_blocks(lens):
    return sum(block_counts(lens))


def over_chunks(body, carry, comp_rows, prompt_rows, slot):
    per_prompt, per_comp = CHUNK // PROWS, CHUNK // BUCKET

    for low in range(0, PROMPT, CHUNK):
        rows = slice(low, low + CHUNK)
        carry = body(rows, rows, prompt_rows(low // PROWS, per_prompt), None, carry)
    for low in range(0, LMAX, CHUNK):
        rows = slice(PROMPT + low, PROMPT + low + CHUNK)
        acc_rows = slice(low, low + CHUNK)
        carry = body(rows, acc_rows, comp_rows(slot * 8 + low // BUCKET, per_comp), low, carry)
    return carry


def put_blocks(o_ref, first, slots, slot, factor=None):
    rows = slots[slot] if factor is None else slots[slot] * factor
    o_ref[pl.ds(slot * 8, 8), first : first + BUCKET, :] = (
        rows.astype(jnp.bfloat16).reshape(8, BUCKET, HEAD_DIM)
    )


def put_prompt(o_ref, first, rows, factor=None):
    rows = rows[...] if factor is None else rows[...] * factor
    o_ref[:, first : first + PROWS, :] = rows.astype(jnp.bfloat16).reshape(HEADS, PROWS, HEAD_DIM)


def split_copies(source, target, sems, count):
    size = source.shape[0] // count
    return [
        pltpu.make_async_copy(
            source.at[pl.ds(part * size, size)], target.at[pl.ds(part * size, size)], sems.at[part]
        )
        for part in range(count)
    ]


def start_all(copies):
    for copy in copies:
        copy.start()


def wait_all(copies):
    for copy in copies:
        copy.wait()


class Loads:
    def __init__(self, source, target, sems, low, high):
        self.source, self.target, self.sems, self.low, self.high = source, target, sems, low, high

    def copy(self, index, *place):
        return pltpu.make_async_copy(
            self.source.at[place], self.target.at[place], self.sems.at[index]
        )

    def prompt(self):
        return self.copy(COMP, slice(None), pl.ds(self.low, self.high - self.low))

    def slot(self, slot):
        first = slot * 8 if isinstance(slot, int) else pl.multiple_of(slot * 8, 8)
        return self.copy(slot, pl.ds(first, 8), pl.ds(0, self.low))

    def start(self):
        self.prompt().start()
        for slot in range(COMP):
            self.slot(slot).start()


def prob_kernel(
    len_ref, x_hbm, p_hbm, o_hbm, x_ref, stage, o_ref, s_ref, e_ref, acc_p, acc_c, top_ref, inv_ref,
    in_sems, p_sems, o_sems
):
    load = Loads(x_hbm, x_ref, in_sems, KP0, ROWS1)
    load.start()
    blocks = live_blocks(len_ref)
    for ref in (acc_p, acc_c):
        ref[...] = jnp.zeros_like(ref)
    load.prompt().wait()
    load.slot(0).wait()
    store = Loads(o_ref, o_hbm, o_sems, DVP0, ROWS3)

    def save(index):
        slot = lax.rem(index, 2)
        return split_copies(stage.at[slot], p_hbm.at[index], p_sems.at[slot], PARTS)

    def run(step, score, exponent, weigh):
        slot, place = locate(len_ref, step)
        old_slot, old_place = locate(len_ref, step - 2)
        old = lax.rem(step, 2)
        length = len_ref[slot]
        queries = rows_of(x_ref, slot * 8 + place * (QB // BUCKET), QB // BUCKET, Q0, Q0 + BUCKET)
        grad_out = rows_of(
            x_ref, old_slot * 8 + old_place * (QB // BUCKET), QB // BUCKET, D0, D0 + BUCKET
        )
        top = top_ref[0:1, :]
        inverse = inv_ref[0:1, :]

        def body(rows, acc_rows, keys, low, carry):
            peak, total = carry
            if weigh:
                prob = (e_ref[rows, :] * inverse).astype(jnp.bfloat16)
                stage[old, rows, :] = prob
                grad = dot(prob, grad_out, NN)
                if low is None:
                    acc_p[acc_rows, :] += grad
                else:
                    acc_c[old_slot, acc_rows, :] += grad
            if exponent:
                expo = jnp.exp2(s_ref[rows, :] - top)
                e_ref[rows, :] = expo
                total = total + fold(expo, jnp.sum)
            if score:
                scores = dot(keys, queries, NT) * (TEMPER * LOG2E)
                if low is not None:
                    parts = []
                    for part in range(0, CHUNK, BUCKET):
                        seen = low + part < length
                        parts.append(jnp.where(seen, scores[part : part + BUCKET], HIDDEN))
                    scores = jnp.concatenate(parts, axis=0)
                s_ref[rows, :] = scores
                peak = jnp.maximum(peak, fold(scores, jnp.max))
            return peak, total

        peak, total = over_chunks(
            body,
            (jnp.full((FOLD, QB), HIDDEN, jnp.float32), jnp.zeros((FOLD, QB), jnp.float32)),
            lambda first, count: rows_of(x_ref, first, count, K0, K0 + BUCKET),
            lambda first, count: rows_of(x_ref, first, count, KP0, KP0 + PROWS),
            slot,
        )
        if score:
            top_ref[0:1, :] = jnp.max(peak, axis=0, keepdims=True)
        if exponent:
            inv_ref[0:1, :] = 1.0 / jnp.sum(total, axis=0, keepdims=True)

    run(0, True, False, False)
    for slot in range(1, COMP):
        load.slot(slot).wait()
    run(1, True, True, False)

    @pl.loop(2, blocks)
    def _(step):
        @pl.when(step >= 4)
        def _():
            wait_all(save(step - 4))

        run(step, True, True, True)
        start_all(save(step - 2))

    wait_all(save(blocks - 4))
    run(blocks, False, True, True)
    start_all(save(blocks - 2))
    wait_all(save(blocks - 3))
    run(blocks + 1, False, False, True)
    start_all(save(blocks - 1))
    put_prompt(o_ref, DVP0, acc_p)
    store.prompt().start()
    for slot in range(COMP):
        put_blocks(o_ref, DV0, acc_c, slot)
        store.slot(slot).start()
    wait_all(save(blocks - 2))
    wait_all(save(blocks - 1))
    store.prompt().wait()
    for slot in range(COMP):
        store.slot(slot).wait()


def score_kernel(
    len_ref, x_hbm, y_hbm, p_hbm, o_hbm, x_ref, y_ref, p_ref, o_ref, d_ref, acc_p, acc_c, dq_ref,
    kpt_ref, kct_ref, delta_ref, x_sems, y_sems, p_sems, o_sems
):
    load_x = Loads(x_hbm, x_ref, x_sems, KP0, ROWS1)
    load_y = Loads(y_hbm, y_ref, y_sems, VP0, CNT0)
    store = Loads(o_ref, o_hbm, o_sems, DKP0, ROWS4)

    def fetch(index):
        slot = lax.rem(index, 3)
        return split_copies(p_hbm.at[index], p_ref.at[slot], p_sems.at[slot], PARTS)

    load_y.prompt().start()
    load_y.slot(0).start()
    load_x.slot(0).start()
    start_all(fetch(0))
    load_x.prompt().start()
    for slot in range(1, COMP):
        load_y.slot(slot).start()
        load_x.slot(slot).start()
    start_all(fetch(1))
    blocks = live_blocks(len_ref)
    o_ref[:, DQ0 : DQ0 + BUCKET, :] = jnp.zeros((HEADS, BUCKET, HEAD_DIM), jnp.bfloat16)
    for ref in (acc_p, acc_c):
        ref[...] = jnp.zeros_like(ref)
    load_y.prompt().wait()

    def admit(slot):
        load_y.slot(slot).wait()
        load_x.slot(slot).wait()
        kct_ref[slot] = rows_of(x_ref, slot * 8, 8, K0, K0 + BUCKET).T

    def run(step, probe, spread):
        slot, place = locate(len_ref, step)
        old_slot, old_place = locate(len_ref, step - 1)
        now = lax.rem(step, 3)
        old = lax.rem(step + 2, 3)
        grad_out = rows_of(x_ref, slot * 8 + place * (QB // BUCKET), QB // BUCKET, D0, D0 + BUCKET)
        old_first = old_slot * 8 + old_place * (QB // BUCKET)
        queries = rows_of(x_ref, old_first, QB // BUCKET, Q0, Q0 + BUCKET)
        delta = delta_ref[0:1, :]
        if spread:
            dq_ref[...] = jnp.zeros_like(dq_ref)

        def body(rows, acc_rows, values, low, partial):
            if spread:
                grad_s = (
                    p_ref[old, rows, :].astype(jnp.float32) * (d_ref[rows, :] - delta)
                ).astype(jnp.bfloat16)
                grad = dot(grad_s, queries, NN)
                if low is None:
                    acc_p[acc_rows, :] += grad
                    dq_ref[...] += dot(kpt_ref[:, acc_rows], grad_s, NN)
                else:
                    acc_c[old_slot, acc_rows, :] += grad
                    dq_ref[...] += dot(kct_ref[old_slot, :, acc_rows], grad_s, NN)
            if probe:
                grad_prob = dot(values, grad_out, NT)
                d_ref[rows, :] = grad_prob
                partial = partial + fold(p_ref[now, rows, :].astype(jnp.float32) * grad_prob, jnp.sum)
            return partial

        partial = over_chunks(
            body,
            jnp.zeros((FOLD, QB), jnp.float32),
            lambda first, count: rows_of(y_ref, first, count, V0, V0 + BUCKET),
            lambda first, count: rows_of(y_ref, first, count, VP0, VP0 + PROWS),
            slot,
        )
        if probe:
            delta_ref[0:1, :] = jnp.sum(partial, axis=0, keepdims=True)
        if spread:
            o_ref[pl.ds(old_first, QB // BUCKET), DQ0 : DQ0 + BUCKET, :] = (
                (dq_ref[...].T * TEMPER).astype(jnp.bfloat16).reshape(QB // BUCKET, BUCKET, HEAD_DIM)
            )

    admit(0)
    wait_all(fetch(0))
    run(0, True, False)
    load_x.prompt().wait()
    kpt_ref[...] = rows_of(x_ref, 0, HEADS, KP0, KP0 + PROWS).T
    for slot in range(1, COMP):
        admit(slot)

    @pl.loop(1, blocks)
    def _(step):
        @pl.when(step + 1 < blocks)
        def _():
            start_all(fetch(step + 1))

        wait_all(fetch(step))
        run(step, True, True)

    run(blocks, False, True)
    put_prompt(o_ref, DKP0, acc_p, TEMPER)
    store.prompt().start()
    for slot in range(COMP):
        put_blocks(o_ref, DK0, acc_c, slot, TEMPER)
        store.slot(slot).start()
    store.prompt().wait()
    for slot in range(COMP):
        store.slot(slot).wait()


MAX_BLOCKS = COMP * QSTEPS
PRODUCT = 2 * COMP * LMAX * KEYS * HEAD_DIM
FAR = pl.BlockSpec(memory_space=pltpu.HBM)
SCALARS = pl.BlockSpec(memory_space=pltpu.SMEM)


def sems(*shape):
    return pltpu.SemaphoreType.DMA(shape)


def blocks_of(rows):
    return (HEADS, rows, HEAD_DIM)


def run_prob(lengths, first):
    return pl.pallas_call(
        prob_kernel,
        in_specs=[SCALARS, FAR],
        out_specs=[FAR, FAR],
        scratch_shapes=[
            pltpu.VMEM(blocks_of(ROWS1), jnp.bfloat16),
            pltpu.VMEM((2, KEYS, QB), jnp.bfloat16),
            pltpu.VMEM(blocks_of(ROWS3), jnp.bfloat16),
            pltpu.VMEM((KEYS, QB), jnp.float32),
            pltpu.VMEM((KEYS, QB), jnp.float32),
            pltpu.VMEM((PROMPT, HEAD_DIM), jnp.float32),
            pltpu.VMEM((COMP, LMAX, HEAD_DIM), jnp.float32),
            pltpu.VMEM((8, QB), jnp.float32),
            pltpu.VMEM((8, QB), jnp.float32),
            sems(COMP + 1),
            sems(2, PARTS),
            sems(COMP + 1),
        ],
        out_shape=[
            jax.ShapeDtypeStruct((MAX_BLOCKS, KEYS, QB), jnp.bfloat16),
            jax.ShapeDtypeStruct(blocks_of(ROWS3), jnp.bfloat16),
        ],
        compiler_params=pltpu.CompilerParams(vmem_limit_bytes=VMEM_LIMIT),
        cost_estimate=pl.CostEstimate(
            flops=2 * PRODUCT, bytes_accessed=30 * 2**20, transcendentals=COMP * LMAX * KEYS
        ),
        name="attn_prob",
    )(lengths, first)


def run_score(lengths, first, second, prob):
    return pl.pallas_call(
        score_kernel,
        in_specs=[SCALARS, FAR, FAR, FAR],
        out_specs=FAR,
        scratch_shapes=[
            pltpu.VMEM(blocks_of(ROWS1), jnp.bfloat16),
            pltpu.VMEM(blocks_of(ROWS2), jnp.bfloat16),
            pltpu.VMEM((3, KEYS, QB), jnp.bfloat16),
            pltpu.VMEM(blocks_of(ROWS4), jnp.bfloat16),
            pltpu.VMEM((KEYS, QB), jnp.float32),
            pltpu.VMEM((PROMPT, HEAD_DIM), jnp.float32),
            pltpu.VMEM((COMP, LMAX, HEAD_DIM), jnp.float32),
            pltpu.VMEM((HEAD_DIM, QB), jnp.float32),
            pltpu.VMEM((HEAD_DIM, PROMPT), jnp.bfloat16),
            pltpu.VMEM((COMP, HEAD_DIM, LMAX), jnp.bfloat16),
            pltpu.VMEM((8, QB), jnp.float32),
            sems(COMP + 1),
            sems(COMP + 1),
            sems(3, PARTS),
            sems(COMP + 1),
        ],
        out_shape=jax.ShapeDtypeStruct(blocks_of(ROWS4), jnp.bfloat16),
        compiler_params=pltpu.CompilerParams(vmem_limit_bytes=VMEM_LIMIT),
        cost_estimate=pl.CostEstimate(
            flops=3 * PRODUCT, bytes_accessed=30 * 2**20, transcendentals=0
        ),
        name="grad_scores",
    )(lengths, first, second, prob)


WIDE = 8


def pack_kernel(
    len_hbm, gain_hbm, mask_hbm, q_hbm, k_hbm, c_hbm, kp_hbm, o_hbm,
    len_ref, gain_ref, mask_ref, q_ref, k_ref, c_ref, kp_ref, o_ref, factor_ref,
    few_sems, in_sems, out_sems
):
    few = [
        pltpu.make_async_copy(source, target, few_sems.at[index])
        for index, (source, target) in enumerate(
            ((len_hbm, len_ref), (gain_hbm, gain_ref), (mask_hbm, mask_ref))
        )
    ]
    start_all(few)
    width = WIDE * HEAD_DIM
    pairs = ((q_hbm, q_ref), (k_hbm, k_ref), (c_hbm, c_ref), (kp_hbm, kp_ref))
    loads, stores = [], []
    for part in range(HEADS // WIDE):
        lanes = pl.ds(part * width, width)
        loads.append(
            [
                pltpu.make_async_copy(
                    source.at[0, :, lanes], target.at[:, lanes], in_sems.at[part, index]
                )
                for index, (source, target) in enumerate(pairs)
            ]
        )
        heads = pl.ds(part * WIDE, WIDE)
        stores.append(pltpu.make_async_copy(o_ref.at[heads], o_hbm.at[heads], out_sems.at[part]))
        start_all(loads[-1])
    wait_all(few)
    me = lax.axis_index("seq")
    slot = lax.div(me, LMAX // BUCKET)
    place = (me - slot * (LMAX // BUCKET)) * BUCKET
    live = (mask_ref[...] * (place < len_ref[0, slot]).astype(jnp.int32)).astype(jnp.float32)
    factor_ref[...] = jnp.broadcast_to(live * gain_ref[0, slot], (HEAD_DIM, BUCKET)).T
    for part in range(HEADS // WIDE):
        wait_all(loads[part])
        for head in range(part * WIDE, part * WIDE + WIDE):
            lanes = slice(head * HEAD_DIM, head * HEAD_DIM + HEAD_DIM)
            o_ref[head, Q0 : Q0 + BUCKET, :] = q_ref[:, lanes]
            o_ref[head, K0 : K0 + BUCKET, :] = k_ref[:, lanes]
            o_ref[head, D0 : D0 + BUCKET, :] = (
                c_ref[:, lanes].astype(jnp.float32) * factor_ref[...]
            ).astype(jnp.bfloat16)
            o_ref[head, KP0 : KP0 + PROWS, :] = kp_ref[:, lanes]
        stores[part].start()
    wait_all(stores)


def wide_rows(rows):
    return pl.BlockSpec((1, rows, WIDE * HEAD_DIM), lambda step, *_: (0, 0, step))


def wide_heads(rows):
    return pl.BlockSpec((WIDE, rows, HEAD_DIM), lambda step, *_: (step, 0, 0))


def run_pack(lengths, gain, mask, queries, keys, cotangent, prompt_keys):
    wide = HEADS * HEAD_DIM
    return pl.pallas_call(
        pack_kernel,
        in_specs=[FAR] * 7,
        out_specs=FAR,
        scratch_shapes=[
            pltpu.SMEM((1, COMP), jnp.int32),
            pltpu.SMEM((1, COMP), jnp.float32),
            pltpu.VMEM((1, BUCKET), jnp.int32),
            pltpu.VMEM((BUCKET, wide), jnp.bfloat16),
            pltpu.VMEM((BUCKET, wide), jnp.bfloat16),
            pltpu.VMEM((BUCKET, wide), jnp.bfloat16),
            pltpu.VMEM((PROWS, wide), jnp.bfloat16),
            pltpu.VMEM(blocks_of(ROWS1), jnp.bfloat16),
            pltpu.VMEM((BUCKET, HEAD_DIM), jnp.float32),
            sems(3),
            sems(HEADS // WIDE, 4),
            sems(HEADS // WIDE),
        ],
        out_shape=jax.ShapeDtypeStruct(blocks_of(ROWS1), jnp.bfloat16),
        compiler_params=pltpu.CompilerParams(vmem_limit_bytes=VMEM_LIMIT),
        name="pack_first",
    )(lengths, gain, mask, queries, keys, cotangent, prompt_keys)


def run_unpack(name, blocks, scale, parts, limit):
    def kernel(scale_ref, x_ref, *o_refs):
        for head in range(WIDE):
            lanes = slice(head * HEAD_DIM, head * HEAD_DIM + HEAD_DIM)
            for (low, rows), o_ref in zip(parts, o_refs):
                o_ref[0, :, lanes] = (
                    x_ref[head, low : low + rows, :].astype(jnp.float32) * scale_ref[0]
                ).astype(jnp.bfloat16)

    return pl.pallas_call(
        kernel,
        grid_spec=pltpu.PrefetchScalarGridSpec(
            num_scalar_prefetch=1,
            grid=(HEADS // WIDE,),
            in_specs=[wide_heads(blocks.shape[1])],
            out_specs=[wide_rows(rows) for _, rows in parts],
        ),
        out_shape=[
            jax.ShapeDtypeStruct((1, rows, HEADS * HEAD_DIM), jnp.bfloat16) for _, rows in parts
        ],
        compiler_params=pltpu.CompilerParams(
            dimension_semantics=("arbitrary",), vmem_limit_bytes=limit
        ),
        name=name,
    )(scale, blocks)


def to_heads(matrix):
    return matrix.reshape(matrix.shape[0], HEADS, HEAD_DIM).transpose(1, 0, 2)


def exchange(blocks):
    return lax.all_to_all(blocks, "seq", split_axis=0, concat_axis=0, tiled=True)


def on_device(comp_q, comp_k, comp_v, cotangent, prompt_k, prompt_v, lengths, loss_mask, advantage):
    row_count = comp_q.shape[1]
    seq_ways = lax.axis_size("seq")
    grp_ways = lax.axis_size("grp")
    slot_total = lengths.shape[1]
    token_ids = lax.axis_index("seq") * row_count + jnp.arange(row_count, dtype=jnp.int32)
    slot_ids = token_ids // LMAX
    position = token_ids % LMAX
    member = slot_ids[:, None] == jnp.arange(slot_total, dtype=jnp.int32)[None, :]
    token_limit = jnp.sum(jnp.where(member, lengths[0][None, :], 0), axis=1)
    live_weight = (loss_mask[0] * (position < token_limit).astype(jnp.int32)).astype(jnp.float32)
    count = jnp.broadcast_to(
        jnp.sum(live_weight).astype(jnp.bfloat16), (HEADS, ROWS2 - CNT0, HEAD_DIM)
    )
    send_first = run_pack(
        lengths, advantage, loss_mask, comp_q, comp_k, cotangent, prompt_k
    )
    first = exchange(send_first)
    send_second = jnp.concatenate([to_heads(comp_v[0]), to_heads(prompt_v[0]), count], axis=1)
    send_second, first = lax.optimization_barrier((send_second, first))
    second = exchange(send_second)
    prob, send_third = run_prob(lengths[0], first)
    live_total = jnp.sum(second[:, CNT0, 0].astype(jnp.float32)).reshape(1, 1)
    send_third, second = lax.optimization_barrier((send_third, second))
    third = exchange(send_third)
    for other in (1, 2):
        live_total = live_total + lax.ppermute(
            live_total, "grp", [(index, index ^ other) for index in range(grp_ways)]
        )
    loss_scale = grp_ways * seq_ways * row_count / jnp.maximum(live_total[0, 0], 1.0)
    send_fourth = run_score(lengths[0], first, second, prob)
    send_fourth, third = lax.optimization_barrier((send_fourth, third))
    fourth = exchange(send_fourth)

    loss_scale = loss_scale.astype(jnp.float32).reshape(1)
    grad_v, grad_vp = run_unpack("unpack_third", third, loss_scale, ((DV0, BUCKET), (DVP0, PROWS)), 16 * 2**20)
    grad_k, grad_q, grad_kp = run_unpack(
        "unpack_fourth", fourth, loss_scale, ((DK0, BUCKET), (DQ0, BUCKET), (DKP0, PROWS)), 16 * 2**20
    )
    return grad_q, grad_k, grad_v, grad_kp, grad_vp


def solution(mesh):
    return jax.shard_map(
        on_device,
        mesh=mesh,
        in_specs=(
            P("grp", "seq", None),
            P("grp", "seq", None),
            P("grp", "seq", None),
            P("grp", "seq", None),
            P("grp", "seq", None),
            P("grp", "seq", None),
            P("grp", None),
            P("grp", "seq"),
            P("grp", None),
        ),
        out_specs=(
            P("grp", "seq", None),
            P("grp", "seq", None),
            P("grp", "seq", None),
            P("grp", "seq", None),
            P("grp", "seq", None),
        ),
        check_vma=False,
    )
```

```python
import jax
import jax.numpy as jnp
from jax import lax
from jax.experimental import pallas as pl
from jax.experimental.pallas import tpu as pltpu
from jax.sharding import PartitionSpec as P

HEADS = 32
HEAD_DIM = 128
LMAX = 1024
PROMPT = 2048
COMP = 4
BUCKET = 128
PROWS = 64
KEYS = PROMPT + LMAX
QB = 256
QSTEPS = LMAX // QB
CHUNK = 1024
FOLD = 8
VMEM_LIMIT = 63 * 2**20
PARTS = 2
TEMPER = HEAD_DIM ** (-0.5)
LOG2E = 1.4426950408889634
HIDDEN = -1e30

Q0, K0, D0, KP0, ROWS1 = 0, 128, 256, 384, 448
V0, VP0, CNT0, ROWS2 = 0, 128, 192, 200
DV0, DVP0, ROWS3 = 0, 128, 192
DK0, DQ0, DKP0, ROWS4 = 0, 128, 256, 320

NT = (((1,), (1,)), ((), ()))
NN = (((1,), (0,)), ((), ()))


def dot(left, right, dims):
    return lax.dot_general(left, right, dims, preferred_element_type=jnp.float32)


def rows_of(ref, first, count, low, high):
    return ref[pl.ds(first, count), low:high, :].reshape(count * (high - low), HEAD_DIM)


def fold(values, op):
    return op(values.reshape(values.shape[0] // FOLD, FOLD, values.shape[1]), axis=0)


def block_counts(lens):
    return [lax.div(lens[slot] + (QB - 1), QB) for slot in range(COMP)]


def locate(lens, index):
    counts = block_counts(lens)
    ends, end = [], 0
    for count in counts:
        end = end + count
        ends.append(end)
    index = jnp.clip(index, 0, end - 1)
    slot, base = 0, 0
    for place in range(COMP - 1):
        passed = index >= ends[place]
        slot = slot + passed.astype(jnp.int32)
        base = jnp.where(passed, ends[place], base)
    return slot, index - base


def live_blocks(lens):
    return sum(block_counts(lens))


def over_chunks(body, carry, comp_rows, prompt_rows, slot):
    per_prompt, per_comp = CHUNK // PROWS, CHUNK // BUCKET

    for low in range(0, PROMPT, CHUNK):
        rows = slice(low, low + CHUNK)
        carry = body(rows, rows, prompt_rows(low // PROWS, per_prompt), None, carry)
    for low in range(0, LMAX, CHUNK):
        rows = slice(PROMPT + low, PROMPT + low + CHUNK)
        acc_rows = slice(low, low + CHUNK)
        carry = body(rows, acc_rows, comp_rows(slot * 8 + low // BUCKET, per_comp), low, carry)
    return carry


def put_blocks(o_ref, first, slots, slot, factor=None):
    rows = slots[slot] if factor is None else slots[slot] * factor
    o_ref[pl.ds(slot * 8, 8), first : first + BUCKET, :] = (
        rows.astype(jnp.bfloat16).reshape(8, BUCKET, HEAD_DIM)
    )


def put_prompt(o_ref, first, rows, factor=None):
    rows = rows[...] if factor is None else rows[...] * factor
    o_ref[:, first : first + PROWS, :] = rows.astype(jnp.bfloat16).reshape(HEADS, PROWS, HEAD_DIM)


def split_copies(source, target, sems, count):
    size = source.shape[0] // count
    return [
        pltpu.make_async_copy(
            source.at[pl.ds(part * size, size)], target.at[pl.ds(part * size, size)], sems.at[part]
        )
        for part in range(count)
    ]


def start_all(copies):
    for copy in copies:
        copy.start()


def wait_all(copies):
    for copy in copies:
        copy.wait()


class Loads:
    def __init__(self, source, target, sems, low, high):
        self.source, self.target, self.sems, self.low, self.high = source, target, sems, low, high

    def copy(self, index, *place):
        return pltpu.make_async_copy(
            self.source.at[place], self.target.at[place], self.sems.at[index]
        )

    def prompt(self):
        return self.copy(COMP, slice(None), pl.ds(self.low, self.high - self.low))

    def slot(self, slot):
        first = slot * 8 if isinstance(slot, int) else pl.multiple_of(slot * 8, 8)
        return self.copy(slot, pl.ds(first, 8), pl.ds(0, self.low))

    def start(self):
        self.prompt().start()
        for slot in range(COMP):
            self.slot(slot).start()


def prob_kernel(
    len_ref, x_hbm, p_hbm, o_hbm, x_ref, stage, o_ref, s_ref, e_ref, acc_p, acc_c, top_ref, inv_ref,
    in_sems, p_sems, o_sems
):
    load = Loads(x_hbm, x_ref, in_sems, KP0, ROWS1)
    load.start()
    blocks = live_blocks(len_ref)
    for ref in (acc_p, acc_c):
        ref[...] = jnp.zeros_like(ref)
    load.prompt().wait()
    load.slot(0).wait()
    store = Loads(o_ref, o_hbm, o_sems, DVP0, ROWS3)

    def save(index):
        slot = lax.rem(index, 2)
        return split_copies(stage.at[slot], p_hbm.at[index], p_sems.at[slot], PARTS)

    def run(step, score, exponent, weigh):
        slot, place = locate(len_ref, step)
        old_slot, old_place = locate(len_ref, step - 2)
        old = lax.rem(step, 2)
        length = len_ref[slot]
        queries = rows_of(x_ref, slot * 8 + place * (QB // BUCKET), QB // BUCKET, Q0, Q0 + BUCKET)
        grad_out = rows_of(
            x_ref, old_slot * 8 + old_place * (QB // BUCKET), QB // BUCKET, D0, D0 + BUCKET
        )
        top = top_ref[0:1, :]
        inverse = inv_ref[0:1, :]

        def body(rows, acc_rows, keys, low, carry):
            peak, total = carry
            if weigh:
                prob = (e_ref[rows, :] * inverse).astype(jnp.bfloat16)
                stage[old, rows, :] = prob
                grad = dot(prob, grad_out, NN)
                if low is None:
                    acc_p[acc_rows, :] += grad
                else:
                    acc_c[old_slot, acc_rows, :] += grad
            if exponent:
                expo = jnp.exp2(s_ref[rows, :] - top)
                e_ref[rows, :] = expo
                total = total + fold(expo, jnp.sum)
            if score:
                scores = dot(keys, queries, NT) * (TEMPER * LOG2E)
                if low is not None:
                    parts = []
                    for part in range(0, CHUNK, BUCKET):
                        seen = low + part < length
                        parts.append(jnp.where(seen, scores[part : part + BUCKET], HIDDEN))
                    scores = jnp.concatenate(parts, axis=0)
                s_ref[rows, :] = scores
                peak = jnp.maximum(peak, fold(scores, jnp.max))
            return peak, total

        peak, total = over_chunks(
            body,
            (jnp.full((FOLD, QB), HIDDEN, jnp.float32), jnp.zeros((FOLD, QB), jnp.float32)),
            lambda first, count: rows_of(x_ref, first, count, K0, K0 + BUCKET),
            lambda first, count: rows_of(x_ref, first, count, KP0, KP0 + PROWS),
            slot,
        )
        if score:
            top_ref[0:1, :] = jnp.max(peak, axis=0, keepdims=True)
        if exponent:
            inv_ref[0:1, :] = 1.0 / jnp.sum(total, axis=0, keepdims=True)

    run(0, True, False, False)
    for slot in range(1, COMP):
        load.slot(slot).wait()
    run(1, True, True, False)

    @pl.loop(2, blocks)
    def _(step):
        @pl.when(step >= 4)
        def _():
            wait_all(save(step - 4))

        run(step, True, True, True)
        start_all(save(step - 2))

    wait_all(save(blocks - 4))
    run(blocks, False, True, True)
    start_all(save(blocks - 2))
    wait_all(save(blocks - 3))
    run(blocks + 1, False, False, True)
    start_all(save(blocks - 1))
    put_prompt(o_ref, DVP0, acc_p)
    store.prompt().start()
    for slot in range(COMP):
        put_blocks(o_ref, DV0, acc_c, slot)
        store.slot(slot).start()
    wait_all(save(blocks - 2))
    wait_all(save(blocks - 1))
    store.prompt().wait()
    for slot in range(COMP):
        store.slot(slot).wait()


def score_kernel(
    len_ref, x_hbm, y_hbm, p_hbm, o_hbm, x_ref, y_ref, p_ref, o_ref, d_ref, acc_p, acc_c, dq_ref,
    kpt_ref, kct_ref, delta_ref, x_sems, y_sems, p_sems, o_sems
):
    load_x = Loads(x_hbm, x_ref, x_sems, KP0, ROWS1)
    load_y = Loads(y_hbm, y_ref, y_sems, VP0, CNT0)
    store = Loads(o_ref, o_hbm, o_sems, DKP0, ROWS4)

    def fetch(index):
        slot = lax.rem(index, 3)
        return split_copies(p_hbm.at[index], p_ref.at[slot], p_sems.at[slot], PARTS)

    load_y.prompt().start()
    load_y.slot(0).start()
    load_x.slot(0).start()
    start_all(fetch(0))
    load_x.prompt().start()
    for slot in range(1, COMP):
        load_y.slot(slot).start()
        load_x.slot(slot).start()
    start_all(fetch(1))
    blocks = live_blocks(len_ref)
    o_ref[:, DQ0 : DQ0 + BUCKET, :] = jnp.zeros((HEADS, BUCKET, HEAD_DIM), jnp.bfloat16)
    for ref in (acc_p, acc_c):
        ref[...] = jnp.zeros_like(ref)
    load_y.prompt().wait()

    def admit(slot):
        load_y.slot(slot).wait()
        load_x.slot(slot).wait()
        kct_ref[slot] = rows_of(x_ref, slot * 8, 8, K0, K0 + BUCKET).T

    def run(step, probe, spread):
        slot, place = locate(len_ref, step)
        old_slot, old_place = locate(len_ref, step - 1)
        now = lax.rem(step, 3)
        old = lax.rem(step + 2, 3)
        grad_out = rows_of(x_ref, slot * 8 + place * (QB // BUCKET), QB // BUCKET, D0, D0 + BUCKET)
        old_first = old_slot * 8 + old_place * (QB // BUCKET)
        queries = rows_of(x_ref, old_first, QB // BUCKET, Q0, Q0 + BUCKET)
        delta = delta_ref[0:1, :]
        if spread:
            dq_ref[...] = jnp.zeros_like(dq_ref)

        def body(rows, acc_rows, values, low, partial):
            if spread:
                grad_s = (
                    p_ref[old, rows, :].astype(jnp.float32) * (d_ref[rows, :] - delta)
                ).astype(jnp.bfloat16)
                grad = dot(grad_s, queries, NN)
                if low is None:
                    acc_p[acc_rows, :] += grad
                    dq_ref[...] += dot(kpt_ref[:, acc_rows], grad_s, NN)
                else:
                    acc_c[old_slot, acc_rows, :] += grad
                    dq_ref[...] += dot(kct_ref[old_slot, :, acc_rows], grad_s, NN)
            if probe:
                grad_prob = dot(values, grad_out, NT)
                d_ref[rows, :] = grad_prob
                partial = partial + fold(p_ref[now, rows, :].astype(jnp.float32) * grad_prob, jnp.sum)
            return partial

        partial = over_chunks(
            body,
            jnp.zeros((FOLD, QB), jnp.float32),
            lambda first, count: rows_of(y_ref, first, count, V0, V0 + BUCKET),
            lambda first, count: rows_of(y_ref, first, count, VP0, VP0 + PROWS),
            slot,
        )
        if probe:
            delta_ref[0:1, :] = jnp.sum(partial, axis=0, keepdims=True)
        if spread:
            o_ref[pl.ds(old_first, QB // BUCKET), DQ0 : DQ0 + BUCKET, :] = (
                (dq_ref[...].T * TEMPER).astype(jnp.bfloat16).reshape(QB // BUCKET, BUCKET, HEAD_DIM)
            )

    admit(0)
    wait_all(fetch(0))
    run(0, True, False)
    load_x.prompt().wait()
    kpt_ref[...] = rows_of(x_ref, 0, HEADS, KP0, KP0 + PROWS).T
    for slot in range(1, COMP):
        admit(slot)

    @pl.loop(1, blocks)
    def _(step):
        @pl.when(step + 1 < blocks)
        def _():
            start_all(fetch(step + 1))

        wait_all(fetch(step))
        run(step, True, True)

    run(blocks, False, True)
    put_prompt(o_ref, DKP0, acc_p, TEMPER)
    store.prompt().start()
    for slot in range(COMP):
        put_blocks(o_ref, DK0, acc_c, slot, TEMPER)
        store.slot(slot).start()
    store.prompt().wait()
    for slot in range(COMP):
        store.slot(slot).wait()


MAX_BLOCKS = COMP * QSTEPS
PRODUCT = 2 * COMP * LMAX * KEYS * HEAD_DIM
FAR = pl.BlockSpec(memory_space=pltpu.HBM)
SCALARS = pl.BlockSpec(memory_space=pltpu.SMEM)


def sems(*shape):
    return pltpu.SemaphoreType.DMA(shape)


def blocks_of(rows):
    return (HEADS, rows, HEAD_DIM)


def run_prob(lengths, first):
    return pl.pallas_call(
        prob_kernel,
        in_specs=[SCALARS, FAR],
        out_specs=[FAR, FAR],
        scratch_shapes=[
            pltpu.VMEM(blocks_of(ROWS1), jnp.bfloat16),
            pltpu.VMEM((2, KEYS, QB), jnp.bfloat16),
            pltpu.VMEM(blocks_of(ROWS3), jnp.bfloat16),
            pltpu.VMEM((KEYS, QB), jnp.float32),
            pltpu.VMEM((KEYS, QB), jnp.float32),
            pltpu.VMEM((PROMPT, HEAD_DIM), jnp.float32),
            pltpu.VMEM((COMP, LMAX, HEAD_DIM), jnp.float32),
            pltpu.VMEM((8, QB), jnp.float32),
            pltpu.VMEM((8, QB), jnp.float32),
            sems(COMP + 1),
            sems(2, PARTS),
            sems(COMP + 1),
        ],
        out_shape=[
            jax.ShapeDtypeStruct((MAX_BLOCKS, KEYS, QB), jnp.bfloat16),
            jax.ShapeDtypeStruct(blocks_of(ROWS3), jnp.bfloat16),
        ],
        compiler_params=pltpu.CompilerParams(vmem_limit_bytes=VMEM_LIMIT),
        cost_estimate=pl.CostEstimate(
            flops=2 * PRODUCT, bytes_accessed=30 * 2**20, transcendentals=COMP * LMAX * KEYS
        ),
        name="attn_prob",
    )(lengths, first)


def run_score(lengths, first, second, prob):
    return pl.pallas_call(
        score_kernel,
        in_specs=[SCALARS, FAR, FAR, FAR],
        out_specs=FAR,
        scratch_shapes=[
            pltpu.VMEM(blocks_of(ROWS1), jnp.bfloat16),
            pltpu.VMEM(blocks_of(ROWS2), jnp.bfloat16),
            pltpu.VMEM((3, KEYS, QB), jnp.bfloat16),
            pltpu.VMEM(blocks_of(ROWS4), jnp.bfloat16),
            pltpu.VMEM((KEYS, QB), jnp.float32),
            pltpu.VMEM((PROMPT, HEAD_DIM), jnp.float32),
            pltpu.VMEM((COMP, LMAX, HEAD_DIM), jnp.float32),
            pltpu.VMEM((HEAD_DIM, QB), jnp.float32),
            pltpu.VMEM((HEAD_DIM, PROMPT), jnp.bfloat16),
            pltpu.VMEM((COMP, HEAD_DIM, LMAX), jnp.bfloat16),
            pltpu.VMEM((8, QB), jnp.float32),
            sems(COMP + 1),
            sems(COMP + 1),
            sems(3, PARTS),
            sems(COMP + 1),
        ],
        out_shape=jax.ShapeDtypeStruct(blocks_of(ROWS4), jnp.bfloat16),
        compiler_params=pltpu.CompilerParams(vmem_limit_bytes=VMEM_LIMIT),
        cost_estimate=pl.CostEstimate(
            flops=3 * PRODUCT, bytes_accessed=30 * 2**20, transcendentals=0
        ),
        name="grad_scores",
    )(lengths, first, second, prob)


WIDE = 8


def pack_kernel(
    len_hbm, gain_hbm, mask_hbm, q_hbm, k_hbm, c_hbm, kp_hbm, o_hbm,
    len_ref, gain_ref, mask_ref, q_ref, k_ref, c_ref, kp_ref, o_ref, factor_ref,
    few_sems, in_sems, out_sems
):
    few = [
        pltpu.make_async_copy(source, target, few_sems.at[index])
        for index, (source, target) in enumerate(
            ((len_hbm, len_ref), (gain_hbm, gain_ref), (mask_hbm, mask_ref))
        )
    ]
    start_all(few)
    width = WIDE * HEAD_DIM
    pairs = ((q_hbm, q_ref), (k_hbm, k_ref), (c_hbm, c_ref), (kp_hbm, kp_ref))
    loads, stores = [], []
    for part in range(HEADS // WIDE):
        lanes = pl.ds(part * width, width)
        loads.append(
            [
                pltpu.make_async_copy(
                    source.at[0, :, lanes], target.at[:, lanes], in_sems.at[part, index]
                )
                for index, (source, target) in enumerate(pairs)
            ]
        )
        heads = pl.ds(part * WIDE, WIDE)
        stores.append(pltpu.make_async_copy(o_ref.at[heads], o_hbm.at[heads], out_sems.at[part]))
        start_all(loads[-1])
    wait_all(few)
    me = lax.axis_index("seq")
    slot = lax.div(me, LMAX // BUCKET)
    place = (me - slot * (LMAX // BUCKET)) * BUCKET
    live = (mask_ref[...] * (place < len_ref[0, slot]).astype(jnp.int32)).astype(jnp.float32)
    factor_ref[...] = jnp.broadcast_to(live * gain_ref[0, slot], (HEAD_DIM, BUCKET)).T
    for part in range(HEADS // WIDE):
        wait_all(loads[part])
        for head in range(part * WIDE, part * WIDE + WIDE):
            lanes = slice(head * HEAD_DIM, head * HEAD_DIM + HEAD_DIM)
            o_ref[head, Q0 : Q0 + BUCKET, :] = q_ref[:, lanes]
            o_ref[head, K0 : K0 + BUCKET, :] = k_ref[:, lanes]
            o_ref[head, D0 : D0 + BUCKET, :] = (
                c_ref[:, lanes].astype(jnp.float32) * factor_ref[...]
            ).astype(jnp.bfloat16)
            o_ref[head, KP0 : KP0 + PROWS, :] = kp_ref[:, lanes]
        stores[part].start()
    wait_all(stores)


def wide_rows(rows):
    return pl.BlockSpec((1, rows, WIDE * HEAD_DIM), lambda step, *_: (0, 0, step))


def wide_heads(rows):
    return pl.BlockSpec((WIDE, rows, HEAD_DIM), lambda step, *_: (step, 0, 0))


def run_pack(lengths, gain, mask, queries, keys, cotangent, prompt_keys):
    wide = HEADS * HEAD_DIM
    return pl.pallas_call(
        pack_kernel,
        in_specs=[FAR] * 7,
        out_specs=FAR,
        scratch_shapes=[
            pltpu.SMEM((1, COMP), jnp.int32),
            pltpu.SMEM((1, COMP), jnp.float32),
            pltpu.VMEM((1, BUCKET), jnp.int32),
            pltpu.VMEM((BUCKET, wide), jnp.bfloat16),
            pltpu.VMEM((BUCKET, wide), jnp.bfloat16),
            pltpu.VMEM((BUCKET, wide), jnp.bfloat16),
            pltpu.VMEM((PROWS, wide), jnp.bfloat16),
            pltpu.VMEM(blocks_of(ROWS1), jnp.bfloat16),
            pltpu.VMEM((BUCKET, HEAD_DIM), jnp.float32),
            sems(3),
            sems(HEADS // WIDE, 4),
            sems(HEADS // WIDE),
        ],
        out_shape=jax.ShapeDtypeStruct(blocks_of(ROWS1), jnp.bfloat16),
        compiler_params=pltpu.CompilerParams(vmem_limit_bytes=VMEM_LIMIT),
        name="pack_first",
    )(lengths, gain, mask, queries, keys, cotangent, prompt_keys)


def run_unpack(name, blocks, scale, parts, limit):
    def kernel(scale_ref, x_ref, *o_refs):
        for head in range(WIDE):
            lanes = slice(head * HEAD_DIM, head * HEAD_DIM + HEAD_DIM)
            for (low, rows), o_ref in zip(parts, o_refs):
                o_ref[0, :, lanes] = (
                    x_ref[head, low : low + rows, :].astype(jnp.float32) * scale_ref[0]
                ).astype(jnp.bfloat16)

    return pl.pallas_call(
        kernel,
        grid_spec=pltpu.PrefetchScalarGridSpec(
            num_scalar_prefetch=1,
            grid=(HEADS // WIDE,),
            in_specs=[wide_heads(blocks.shape[1])],
            out_specs=[wide_rows(rows) for _, rows in parts],
        ),
        out_shape=[
            jax.ShapeDtypeStruct((1, rows, HEADS * HEAD_DIM), jnp.bfloat16) for _, rows in parts
        ],
        compiler_params=pltpu.CompilerParams(
            dimension_semantics=("arbitrary",), vmem_limit_bytes=limit
        ),
        name=name,
    )(scale, blocks)


def to_heads(matrix):
    return matrix.reshape(matrix.shape[0], HEADS, HEAD_DIM).transpose(1, 0, 2)


def exchange(blocks):
    return lax.all_to_all(blocks, "seq", split_axis=0, concat_axis=0, tiled=True)


def on_device(comp_q, comp_k, comp_v, cotangent, prompt_k, prompt_v, lengths, loss_mask, advantage):
    row_count = comp_q.shape[1]
    seq_ways = lax.axis_size("seq")
    grp_ways = lax.axis_size("grp")
    slot_total = lengths.shape[1]
    token_ids = lax.axis_index("seq") * row_count + jnp.arange(row_count, dtype=jnp.int32)
    slot_ids = token_ids // LMAX
    position = token_ids % LMAX
    member = slot_ids[:, None] == jnp.arange(slot_total, dtype=jnp.int32)[None, :]
    token_limit = jnp.sum(jnp.where(member, lengths[0][None, :], 0), axis=1)
    live_weight = (loss_mask[0] * (position < token_limit).astype(jnp.int32)).astype(jnp.float32)
    count = jnp.broadcast_to(
        jnp.sum(live_weight).astype(jnp.bfloat16), (HEADS, ROWS2 - CNT0, HEAD_DIM)
    )
    send_first = run_pack(
        lengths, advantage, loss_mask, comp_q, comp_k, cotangent, prompt_k
    )
    first = exchange(send_first)
    send_second = jnp.concatenate([to_heads(comp_v[0]), to_heads(prompt_v[0]), count], axis=1)
    send_second, first = lax.optimization_barrier((send_second, first))
    second = exchange(send_second)
    prob, send_third = run_prob(lengths[0], first)
    live_total = jnp.sum(second[:, CNT0, 0].astype(jnp.float32)).reshape(1, 1)
    send_third, second = lax.optimization_barrier((send_third, second))
    third = exchange(send_third)
    for other in (1, 2):
        live_total = live_total + lax.ppermute(
            live_total, "grp", [(index, index ^ other) for index in range(grp_ways)]
        )
    loss_scale = grp_ways * seq_ways * row_count / jnp.maximum(live_total[0, 0], 1.0)
    send_fourth = run_score(lengths[0], first, second, prob)
    send_fourth, third = lax.optimization_barrier((send_fourth, third))
    fourth = exchange(send_fourth)

    loss_scale = loss_scale.astype(jnp.float32).reshape(1)
    grad_v, grad_vp = run_unpack("unpack_third", third, loss_scale, ((DV0, BUCKET), (DVP0, PROWS)), 16 * 2**20)
    grad_k, grad_q, grad_kp = run_unpack(
        "unpack_fourth", fourth, loss_scale, ((DK0, BUCKET), (DQ0, BUCKET), (DKP0, PROWS)), 16 * 2**20
    )
    return grad_q, grad_k, grad_v, grad_kp, grad_vp


def solution(mesh):
    return jax.shard_map(
        on_device,
        mesh=mesh,
        in_specs=(
            P("grp", "seq", None),
            P("grp", "seq", None),
            P("grp", "seq", None),
            P("grp", "seq", None),
            P("grp", "seq", None),
            P("grp", "seq", None),
            P("grp", None),
            P("grp", "seq"),
            P("grp", None),
        ),
        out_specs=(
            P("grp", "seq", None),
            P("grp", "seq", None),
            P("grp", "seq", None),
            P("grp", "seq", None),
            P("grp", "seq", None),
        ),
        check_vma=False,
    )
```
